32 devices in a mesh: fsdp: 4 (over y, x), ctx: 4 (over z), tp: 2 (over core).
Axes of the slice: x: 2, y: 2, z: 4, core: 2. Of those that a mesh axis runs over, the one named last changes fastest.
Arguments:
- block_in: bfloat16 [4, 1024, 2048], P('fsdp', 'ctx'), may hold values from -6 to 6
- span_order: int32 [4, 8], P('fsdp'), may hold values from 0 to 7, each once within a row
- attn_gain: bfloat16 [2048], P(('fsdp', 'ctx')), may hold values from 0.5 to 1.5
- w_query: bfloat16 [2048, 2048], P(('fsdp', 'ctx'), 'tp'), may hold values from -0.125 to 0.125
- w_key: bfloat16 [2048, 2048], P(('fsdp', 'ctx'), 'tp'), may hold values from -0.125 to 0.125
- w_value: bfloat16 [2048, 2048], P(('fsdp', 'ctx'), 'tp'), may hold values from -0.125 to 0.125
- w_out: bfloat16 [2048, 2048], P('tp', ('fsdp', 'ctx')), may hold values from -1.5 to 1.5
- mlp_gain: bfloat16 [2048], P(('fsdp', 'ctx')), may hold values from 0.5 to 1.5
- w_gate: bfloat16 [2048, 8192], P(('fsdp', 'ctx'), 'tp'), may hold values from -0.125 to 0.125
- w_up: bfloat16 [2048, 8192], P(('fsdp', 'ctx'), 'tp'), may hold values from -0.125 to 0.125
- w_down: bfloat16 [8192, 2048], P('tp', ('fsdp', 'ctx')), may hold values from -0.0625 to 0.0625
- clip_limit: float32 [32], P('tp'), may hold values from 3 to 12
- cotangent: bfloat16 [4, 1024, 2048], P('fsdp', 'ctx'), may hold values from -6 to 6
Outputs:
- block_out: bfloat16 [4, 1024, 2048], P('fsdp', 'ctx')
- input_grad: float32 [4, 1024, 2048], P('fsdp', 'ctx')
- grad_attn_gain: float32 [2048], P(('fsdp', 'ctx'))
- grad_w_query: float32 [2048, 2048], P(('fsdp', 'ctx'), 'tp')
- grad_w_key: float32 [2048, 2048], P(('fsdp', 'ctx'), 'tp')
- grad_w_value: float32 [2048, 2048], P(('fsdp', 'ctx'), 'tp')
- grad_w_out: float32 [2048, 2048], P('tp', ('fsdp', 'ctx'))
- grad_mlp_gain: float32 [2048], P(('fsdp', 'ctx'))
- grad_w_gate: float32 [2048, 8192], P(('fsdp', 'ctx'), 'tp')
- grad_w_up: float32 [2048, 8192], P(('fsdp', 'ctx'), 'tp')
- grad_w_down: float32 [8192, 2048], P('tp', ('fsdp', 'ctx'))
- logit_max: float32 [32], P('tp')
- clipped_query: float32 [2048, 2048], P(('fsdp', 'ctx'), 'tp')
- clipped_key: float32 [2048, 2048], P(('fsdp', 'ctx'), 'tp')
The draws below stay inside these ranges and needn't reach their ends.
Inputs may be any that keep to these rules, and one draw needn't show every extreme that they name: Each row is a permutation: slot j of sequence s holds the tokens at positions span_order[s, j] * 128 to span_order[s, j] * 128 + 127.
All inputs are finite; a program needn't handle non-finite values.
Results may differ from the reference program's by a relative error of at most 0.014.
Values may be sent and summed in bfloat16 or wider, within the bound.
No kernel may reach another device: no remote copies, remote signals or barrier semaphores. Data moves between devices by JAX's collectives and lax.ppermute only.
A program may use at most 320 MiB of HBM per device.

```python
import math
import jax
import jax.numpy as jnp
from jax import lax

D = 2048
HEADS = 32
HEAD_DIM = 64
FF = 8192
SPAN = 128
SEQS = 4
LENGTH = 1024
N_CTX = 4


def block_levels(stream_key, shape, pieces, smallest, top_value):
    level, own = 1.0, jax.random.fold_in(stream_key, 6)
    for axis_at, blocks in pieces:
        heights = jnp.exp(jax.random.uniform(jax.random.fold_in(own, axis_at), (blocks,), jnp.float32, smallest / len(pieces), top_value / len(pieces)))
        level = level * jnp.repeat(heights, shape[axis_at] // blocks).reshape([-1 if axis == axis_at else 1 for axis in range(len(shape))])
    return level


def gaussian(rng, shape, width, reach, split=(), held_as=jnp.bfloat16):
    entries = jax.random.normal(rng, shape, jnp.float32) * width
    if len(split) > 0:
        entries = block_levels(rng, shape, split, -0.22, 0.18) * entries
    return jnp.clip(entries, min=-reach, max=reach).astype(held_as)


def setup_inputs(seed: int = 0) -> dict:
    arg_keys = jax.random.split(jax.random.key(seed), 14)
    return {
        "block_in": gaussian(arg_keys[0], (SEQS, LENGTH, D), 1.0, 6.0, ((0, 4), (1, 4))),
        "span_order": jax.vmap(lambda own: jax.random.permutation(own, 2 * N_CTX))(jax.random.split(arg_keys[1], SEQS)).reshape((SEQS, 2 * N_CTX)).astype(jnp.int32),
        "attn_gain": jnp.clip(1.0 + 0.1 * jax.random.normal(arg_keys[2], (D,), jnp.float32), 0.5, 1.5).astype(jnp.bfloat16),
        "w_query": gaussian(arg_keys[3], (D, HEADS * HEAD_DIM), D ** -0.5, 0.125, ((0, 16), (1, 2))),
        "w_key": gaussian(arg_keys[4], (D, HEADS * HEAD_DIM), D ** -0.5, 0.125, ((0, 16), (1, 2))),
        "w_value": gaussian(arg_keys[5], (D, HEADS * HEAD_DIM), D ** -0.5, 0.125, ((0, 16), (1, 2))),
        "w_out": gaussian(arg_keys[6], (HEADS * HEAD_DIM, D), 16 ** -0.5, 1.5, ((0, 2), (1, 16))),
        "mlp_gain": jnp.clip(1.0 + 0.1 * jax.random.normal(arg_keys[7], (D,), jnp.float32), 0.5, 1.5).astype(jnp.bfloat16),
        "w_gate": gaussian(arg_keys[8], (D, FF), D ** -0.5, 0.125, ((0, 16), (1, 2))),
        "w_up": gaussian(arg_keys[9], (D, FF), D ** -0.5, 0.125, ((0, 16), (1, 2))),
        "w_down": gaussian(arg_keys[10], (FF, D), FF ** -0.5, 0.0625, ((0, 2), (1, 16))),
        "clip_limit": jnp.clip(jnp.exp(math.log(12.0) - 1.3862944 * jax.random.uniform(arg_keys[11], (HEADS,), jnp.float32) ** block_levels(arg_keys[11], (HEADS,), ((0, 2),), -0.2, 0.2)), 3.0, 12.0),
        "cotangent": gaussian(arg_keys[12], (SEQS, LENGTH, D), 1.0, 6.0, ((0, 4), (1, 4))),
    }


NORM_EPS = 1e-05
ROPE_BASE = 130000.0

@jax.custom_vjp
def low(v):
    return lax.optimization_barrier(v.astype(jnp.bfloat16)).astype(jnp.float32)

@jax.custom_vjp
def low_back(v):
    return v

def low_keep(v):
    return (low(v), None)

def low_pass(kept, grad):
    return (grad,)

def back_keep(v):
    return (v, None)

def back_low(kept, grad):
    return (low(grad),)
low.defvjp(low_keep, low_pass)
low_back.defvjp(back_keep, back_low)

def product(left, right):
    return jnp.dot(left, right, precision=lax.Precision.HIGHEST)

def span_positions(order_row, span_len):
    slot_count = order_row.shape[0]
    offsets = jnp.arange(span_len, dtype=jnp.int32)
    return (order_row[:, None] * span_len + offsets[None, :]).reshape(slot_count * span_len)

def rope_tables(positions, half_dim):
    step_index = jnp.arange(half_dim, dtype=jnp.float32)
    frequency = jnp.power(ROPE_BASE, -2.0 * step_index / (2 * half_dim))
    angles = positions.astype(jnp.float32)[:, None] * frequency[None, :]
    return (jnp.cos(angles), jnp.sin(angles))

def rotate(tensor, cosine_tab, sine_tab):
    half_dim = tensor.shape[-1] // 2
    first_half, second_half = (tensor[..., :half_dim], tensor[..., half_dim:])
    cosine_b, sine_b = (cosine_tab[:, None, :], sine_tab[:, None, :])
    return jnp.concatenate([first_half * cosine_b - second_half * sine_b, second_half * cosine_b + first_half * sine_b], -1)

def block_forward(inputs, positions, gain_one, query_w, key_w, value_w, out_w, gain_two, gate_w, up_w, down_w):
    length = inputs.shape[0]
    heads = query_w.shape[1] // HEAD_DIM
    score_scale = HEAD_DIM ** (-0.5)
    inv_one = lax.rsqrt(lax.optimization_barrier(jnp.mean(inputs * inputs, -1, keepdims=True)) + NORM_EPS)
    normed_one = low(inputs * inv_one * gain_one)
    cosine_tab, sine_tab = rope_tables(positions, HEAD_DIM // 2)
    query_proj = low_back(product(normed_one, query_w))
    key_proj = low_back(product(normed_one, key_w))
    value_proj = low_back(product(normed_one, value_w))
    query_rot = low(rotate(query_proj.reshape(length, heads, HEAD_DIM), cosine_tab, sine_tab))
    key_rot = low(rotate(key_proj.reshape(length, heads, HEAD_DIM), cosine_tab, sine_tab))
    value_low = low(value_proj).reshape(length, heads, HEAD_DIM)
    group_size = math.gcd(heads, 4)
    group_count = heads // group_size

    def split_heads(tensor):
        return tensor.reshape(length, group_count, group_size, HEAD_DIM).transpose(1, 0, 2, 3)
    causal_mask = positions[None, :] <= positions[:, None]

    def head_block(operands):
        query_grp, key_grp, value_grp = operands
        scores = low_back(jnp.einsum('qhd,khd->hqk', query_grp, key_grp, precision=lax.Precision.HIGHEST) * score_scale)
        masked = jnp.where(causal_mask[None], scores, -1e+30)
        head_max = lax.optimization_barrier(jnp.max(masked, axis=(1, 2)))
        row_max = lax.optimization_barrier(jnp.max(masked, axis=2, keepdims=True))
        exp_terms = jnp.exp(masked - row_max)
        probabilities = low(exp_terms / lax.optimization_barrier(jnp.sum(exp_terms, axis=2, keepdims=True)))
        attended = jnp.einsum('hqk,khd->qhd', probabilities, value_grp, precision=lax.Precision.HIGHEST)
        return (attended, head_max)
    attended, head_max = lax.map(jax.checkpoint(head_block), (split_heads(query_rot), split_heads(key_rot), split_heads(value_low)))
    attn_low = low(low_back(attended.transpose(1, 0, 2, 3).reshape(length, heads * HEAD_DIM)))
    resid = inputs + low_back(product(attn_low, out_w))
    inv_two = lax.rsqrt(lax.optimization_barrier(jnp.mean(resid * resid, -1, keepdims=True)) + NORM_EPS)
    normed_two = low(resid * inv_two * gain_two)
    gate_act = low_back(product(normed_two, gate_w))
    up_act = low_back(product(normed_two, up_w))
    hidden = low(jax.nn.silu(gate_act) * up_act)
    block_out = resid + product(hidden, down_w)
    return (block_out, head_max.reshape(heads))

def reference(block_in, span_order, attn_gain, w_query, w_key, w_value, w_out, mlp_gain, w_gate, w_up, w_down, clip_limit, cotangent):
    params = tuple((tensor.astype(jnp.float32) for tensor in (attn_gain, w_query, w_key, w_value, w_out, mlp_gain, w_gate, w_up, w_down)))

    def one_sequence(carry, operands):
        grad_totals, peak = carry
        inputs, order_row, grad_top = operands
        positions = span_positions(order_row, SPAN)

        def wrapped(inputs_full, *weights_all):
            return block_forward(inputs_full, positions, *weights_all)
        block_out, pullback, head_max = jax.vjp(wrapped, inputs.astype(jnp.float32), *params, has_aux=True)
        grads = pullback(grad_top.astype(jnp.float32))
        new_totals = tuple((earlier + addend for earlier, addend in zip(grad_totals, grads[1:])))
        return ((new_totals, jnp.maximum(peak, head_max)), (block_out.astype(jnp.bfloat16), grads[0]))
    start_carry = (tuple((jnp.zeros_like(tensor) for tensor in params)), jnp.full((HEADS,), -1e+30, jnp.float32))
    (totals, peak), (block_out, input_grad) = lax.scan(one_sequence, start_carry, (block_in, span_order, cotangent))
    factor = jnp.sqrt(clip_limit / jnp.maximum(clip_limit, peak))
    column_factor = jnp.repeat(factor, HEAD_DIM)
    clipped_query = w_query.astype(jnp.float32) * column_factor[None, :]
    clipped_key = w_key.astype(jnp.float32) * column_factor[None, :]
    return (block_out, input_grad, totals[0], totals[1], totals[2], totals[3], totals[4], totals[5], totals[6], totals[7], totals[8], peak, clipped_query, clipped_key)
```

```python
import jax
import jax.numpy as jnp
from jax import lax
from jax.sharding import PartitionSpec as P

HEAD_DIM = 64
NORM_EPS = 1e-05
ROPE_BASE = 130000.0

f32 = jnp.float32
bf16 = jnp.bfloat16


def rope_tables(positions, half_dim):
    step_index = jnp.arange(half_dim, dtype=f32)
    frequency = jnp.power(ROPE_BASE, -2.0 * step_index / (2 * half_dim))
    angles = positions.astype(f32)[:, None] * frequency[None, :]
    return (jnp.cos(angles), jnp.sin(angles))


def rotate(tensor, cosine_tab, sine_tab):
    half_dim = tensor.shape[-1] // 2
    first_half, second_half = (tensor[..., :half_dim], tensor[..., half_dim:])
    cosine_b, sine_b = (cosine_tab[:, None, :], sine_tab[:, None, :])
    return jnp.concatenate(
        [
            first_half * cosine_b - second_half * sine_b,
            second_half * cosine_b + first_half * sine_b,
        ],
        -1,
    )


def dot(left, right):
    return jnp.dot(left, right, preferred_element_type=f32)


def dot_lt(left, right):
    return lax.dot_general(left, right, (((0,), (0,)), ((), ())), preferred_element_type=f32)


def dot_rt(left, right):
    return lax.dot_general(left, right, (((1,), (1,)), ((), ())), preferred_element_type=f32)


def on_device(
    block_in,
    span_order,
    attn_gain,
    w_query,
    w_key,
    w_value,
    w_out,
    mlp_gain,
    w_gate,
    w_up,
    w_down,
    clip_limit,
    cotangent,
):
    n_ctx = lax.axis_size("ctx")
    n_fsdp = lax.axis_size("fsdp")
    n_bits = n_fsdp.bit_length() - 1
    c_at = lax.axis_index("ctx")
    f_at = lax.axis_index("fsdp")
    t_at = lax.axis_index("tp")
    row_count, width = block_in.shape[1:]
    span_len = row_count // 2
    feature_block = width // n_fsdp
    score_scale = HEAD_DIM ** (-0.5)

    def along(tensor, shift):
        if shift % n_ctx == 0:
            return tensor
        return lax.ppermute(tensor, "ctx", [(i, (i + shift) % n_ctx) for i in range(n_ctx)])

    def across(tensor, mask):
        return lax.ppermute(tensor, "fsdp", [(i, i ^ mask) for i in range(n_fsdp)])

    def twin(tensor):
        return lax.ppermute(tensor, "tp", [(0, 1), (1, 0)])

    def bit_order(part):
        return [1 << ((part + step) % n_bits) for step in range(n_bits)]

    def part_count(size):
        return n_bits if size % n_bits == 0 else 1

    def reorder(tensor):
        return jnp.concatenate(
            [
                lax.dynamic_slice_in_dim(tensor, (f_at ^ m) * feature_block, feature_block, -1)
                for m in range(n_fsdp)
            ],
            -1,
        )

    def swap_ctx(tensor, split_axis, place_axis):
        piece = tensor.shape[split_axis] // n_ctx
        length = tensor.shape[place_axis]
        shape = list(tensor.shape)
        shape[split_axis] = piece
        shape[place_axis] = length * n_ctx
        placed = jnp.zeros(shape, tensor.dtype)
        for shift in range(n_ctx):
            sent = lax.dynamic_slice_in_dim(
                tensor, ((c_at + shift) % n_ctx) * piece, piece, split_axis
            )
            came = along(sent, shift)
            placed = lax.dynamic_update_slice_in_dim(
                placed, came, ((c_at - shift) % n_ctx) * length, place_axis
            )
        return placed

    def swap_ctx_low(tensor, split_axis, place_axis):
        piece = tensor.shape[split_axis] // n_ctx
        length = tensor.shape[place_axis]
        shape = list(tensor.shape)
        shape[split_axis] = piece
        shape[place_axis] = length * n_ctx
        placed = jnp.zeros(shape, f32)
        for shift in range(n_ctx):
            sent = lax.dynamic_slice_in_dim(
                tensor, ((c_at + shift) % n_ctx) * piece, piece, split_axis
            )
            came = along(sent.astype(bf16), shift).astype(f32) if shift else sent
            placed = lax.dynamic_update_slice_in_dim(
                placed, came, ((c_at - shift) % n_ctx) * length, place_axis
            )
        return placed

    def gather_plane(tensor, axis):
        other = 1 - axis
        parts = part_count(tensor.shape[other])
        part_size = tensor.shape[other] // parts
        done = []
        for part in range(parts):
            held = {0: lax.slice_in_dim(tensor, part * part_size, (part + 1) * part_size, axis=other)}
            for bit in bit_order(part):
                keys = sorted(held)
                came = across(jnp.concatenate([held[k] for k in keys], axis) if len(keys) > 1 else held[keys[0]], bit)
                size = tensor.shape[axis]
                for at, k in enumerate(keys):
                    held[k ^ bit] = lax.slice_in_dim(came, at * size, (at + 1) * size, axis=axis)
            done.append(jnp.concatenate([held[m] for m in range(n_fsdp)], axis))
        return jnp.concatenate(done, other)

    def scatter_plane(tensor, axis):
        other = 1 - axis
        parts = part_count(tensor.shape[other])
        part_size = tensor.shape[other] // parts
        size = tensor.shape[axis] // n_fsdp
        done = []
        for part in range(parts):
            own = lax.slice_in_dim(tensor, part * part_size, (part + 1) * part_size, axis=other)
            held = {m: lax.slice_in_dim(own, m * size, (m + 1) * size, axis=axis) for m in range(n_fsdp)}
            for bit in bit_order(part):
                kept = [m for m in sorted(held) if not m & bit]
                sent = [held[m | bit].astype(bf16) for m in kept]
                came = across(jnp.concatenate(sent, axis) if len(sent) > 1 else sent[0], bit)
                held = {
                    m: held[m] + lax.slice_in_dim(came, at * size, (at + 1) * size, axis=axis).astype(f32)
                    for at, m in enumerate(kept)
                }
            done.append(held[0])
        return jnp.concatenate(done, other)

    def gather_tokens(own):
        spans, held = [], own
        for step in range(n_ctx):
            if step:
                held = along(held, 1)
            spans += [held, twin(held)]
        return jnp.concatenate(spans, 0)

    def scatter_tokens(partial):
        spans = partial.reshape(n_ctx, 2, span_len, width)
        total = None
        for slot in list(range(1, n_ctx)) + [0]:
            mine = spans[slot, 0] + twin(spans[slot, 1].astype(bf16)).astype(f32)
            total = mine if total is None else mine + along(total.astype(bf16), 1).astype(f32)
        return total

    order_row = span_order[0]
    slot_spans = jnp.stack(
        [order_row[2 * ((c_at - s) % n_ctx) + (t_at ^ u)] for s in range(n_ctx) for u in range(2)]
    )
    positions = (
        slot_spans[:, None] * span_len + jnp.arange(span_len, dtype=jnp.int32)[None, :]
    ).reshape(-1)
    causal_mask = positions[None, :] <= positions[:, None]
    cosine, sine = rope_tables(positions, HEAD_DIM // 2)
    length = positions.shape[0]

    def own_rows(tensor):
        return reorder(lax.dynamic_slice_in_dim(tensor[0], t_at * span_len, span_len, 0))

    inputs_own = own_rows(block_in)
    cot_own = own_rows(cotangent)

    inputs_low = gather_tokens(inputs_own)

    gains = jnp.stack([attn_gain, mlp_gain])
    gains = gather_plane_small(swap_small(gains, along, c_at, n_ctx), across, n_bits)
    gain_one, gain_two = gains[0].astype(f32), gains[1].astype(f32)

    heads_width = w_query.shape[1] // n_ctx
    qkv = jnp.stack([w_query, w_key, w_value], 1)
    rows_here = w_query.shape[0]
    qkv = qkv.reshape(rows_here, 3, n_ctx, heads_width).transpose(0, 2, 1, 3).reshape(rows_here, -1)
    qkv_full = gather_plane(swap_ctx(qkv, 1, 0), 0)
    out_full = gather_plane(swap_ctx(w_out, 0, 1), 1)
    gate_full = gather_plane(swap_ctx(w_gate, 1, 0), 0)
    up_full = gather_plane(swap_ctx(w_up, 1, 0), 0)
    down_full = gather_plane(swap_ctx(w_down, 0, 1), 1)
    cot_all = gather_tokens(cot_own)

    inputs = inputs_low.astype(f32)
    inv_one = lax.rsqrt(jnp.mean(inputs * inputs, -1, keepdims=True) + NORM_EPS)
    normed_one = (inputs * inv_one * gain_one).astype(bf16)
    heads_here = heads_width // HEAD_DIM
    proj = dot(normed_one, qkv_full)

    def heads_first(tensor):
        return tensor.reshape(length, heads_here, HEAD_DIM).transpose(1, 0, 2)

    def heads_last(tensor):
        return tensor.transpose(1, 0, 2).reshape(length, heads_width)

    def turned(tensor, sine_tab):
        return rotate(tensor.reshape(length, heads_here, HEAD_DIM), cosine, sine_tab)

    query = turned(proj[:, :heads_width], sine).astype(bf16).transpose(1, 0, 2)
    key = turned(proj[:, heads_width : 2 * heads_width], sine).astype(bf16).transpose(1, 0, 2)
    value = heads_first(proj[:, 2 * heads_width :].astype(bf16))

    def forward_head(operands):
        query_h, key_h, value_h = operands
        scores = dot_rt(query_h, key_h) * score_scale
        masked = jnp.where(causal_mask, scores, -1e30)
        row_max = jnp.max(masked, axis=1, keepdims=True)
        exp_terms = jnp.exp(masked - row_max)
        row_total = jnp.sum(exp_terms, axis=1, keepdims=True)
        attended = dot((exp_terms / row_total).astype(bf16), value_h)
        return (attended.astype(bf16), row_max[:, 0] + jnp.log(row_total[:, 0]), jnp.max(row_max))

    attended, log_total, head_max = lax.map(forward_head, (query, key, value))
    attn_low = heads_last(attended)
    attn_sum = scatter_tokens(dot(attn_low, out_full))

    peak = head_max
    for step in range(n_bits):
        peak = jnp.maximum(peak, across(peak, 1 << step))
    head_peak = jnp.zeros((n_ctx * heads_here,), f32)
    for shift in range(n_ctx):
        head_peak = lax.dynamic_update_slice_in_dim(
            head_peak, along(peak, shift), ((c_at - shift) % n_ctx) * heads_here, 0
        )

    inputs_mine = inputs_own.astype(f32)
    resid = inputs_mine + attn_sum
    inv_two = lax.rsqrt(jnp.mean(resid * resid, -1, keepdims=True) + NORM_EPS)
    scaled_two = resid * inv_two
    normed_two = gather_tokens((scaled_two * gain_two).astype(bf16))
    gate_act = dot(normed_two, gate_full)
    up_act = dot(normed_two, up_full)
    sig_gate = jax.nn.sigmoid(gate_act)
    silu_gate = gate_act * sig_gate
    hidden = (silu_gate * up_act).astype(bf16)
    grad_hidden = dot_rt(cot_all, down_full)
    silu_slope = sig_gate * (1.0 + gate_act * (1.0 - sig_gate))
    grad_gate = (grad_hidden * up_act * silu_slope).astype(bf16)
    grad_up = (grad_hidden * silu_gate).astype(bf16)
    grad_normed_two = scatter_tokens(dot_rt(grad_gate, gate_full) + dot_rt(grad_up, up_full))
    mlp_sum = scatter_tokens(dot(hidden, down_full))
    block_out_mine = (resid + mlp_sum).astype(bf16)

    grad_gain_two = jnp.sum(grad_normed_two * scaled_two, axis=0)
    weighted_two = grad_normed_two * gain_two
    grad_resid = cot_own.astype(f32) + inv_two * (
        weighted_two - scaled_two * jnp.mean(weighted_two * scaled_two, -1, keepdims=True)
    )
    grad_low = gather_tokens(grad_resid.astype(bf16))

    def own_weight(grad, axis):
        return swap_ctx_low(scatter_plane(grad, axis), axis, 1 - axis)

    down_out = own_weight(dot_lt(hidden, cot_all), 1)
    gate_out = own_weight(dot_lt(normed_two, grad_gate), 0)
    up_out = own_weight(dot_lt(normed_two, grad_up), 0)

    grad_attended = heads_first(dot_rt(grad_low, out_full).astype(bf16))
    out_proj_out = own_weight(dot_lt(attn_low, grad_low), 1)

    def backward_head(operands):
        query_h, key_h, value_h, grad_h, log_h = operands
        scores = dot_rt(query_h, key_h) * score_scale
        masked = jnp.where(causal_mask, scores, -1e30)
        probabilities = jnp.exp(masked - log_h[:, None])
        grad_probs = dot_rt(grad_h, value_h)
        row_delta = jnp.sum(probabilities * grad_probs, axis=1, keepdims=True)
        grad_scores = (probabilities * (grad_probs - row_delta)).astype(bf16)
        return (
            dot(grad_scores, key_h) * score_scale,
            dot_lt(grad_scores, query_h) * score_scale,
            dot_lt(probabilities.astype(bf16), grad_h).astype(bf16),
        )

    grad_query, grad_key, grad_value = lax.map(
        backward_head, (query, key, value, grad_attended, log_total)
    )
    grad_proj = jnp.concatenate(
        [
            rotate(grad_query.transpose(1, 0, 2), cosine, -sine).reshape(length, heads_width).astype(bf16),
            rotate(grad_key.transpose(1, 0, 2), cosine, -sine).reshape(length, heads_width).astype(bf16),
            heads_last(grad_value),
        ],
        1,
    )
    grad_normed_one = scatter_tokens(dot_rt(grad_proj, qkv_full))
    grad_qkv = scatter_plane(dot_lt(normed_one, grad_proj), 0)
    query_out, key_out, value_out = (
        swap_ctx_low(grad_qkv[:, i * heads_width : (i + 1) * heads_width], 0, 1) for i in range(3)
    )

    inv_mine = lax.rsqrt(jnp.mean(inputs_mine * inputs_mine, -1, keepdims=True) + NORM_EPS)
    scaled_one = inputs_mine * inv_mine
    grad_gain_one = jnp.sum(grad_normed_one * scaled_one, axis=0)
    weighted_one = grad_normed_one * gain_one
    input_grad_mine = grad_resid + inv_mine * (
        weighted_one - scaled_one * jnp.mean(weighted_one * scaled_one, -1, keepdims=True)
    )

    gain_grads = jnp.stack([grad_gain_one, grad_gain_two])
    gain_grads = gain_grads + twin(gain_grads)
    held = {m: gain_grads[:, m * feature_block : (m + 1) * feature_block] for m in range(n_fsdp)}
    for bit in bit_order(0):
        kept = [m for m in sorted(held) if not m & bit]
        came = across(jnp.concatenate([held[m | bit] for m in kept], 1), bit)
        held = {
            m: held[m] + came[:, at * feature_block : (at + 1) * feature_block]
            for at, m in enumerate(kept)
        }
    piece = feature_block // n_ctx
    gain_total = None
    for shift in range(n_ctx):
        came = along(
            lax.dynamic_slice_in_dim(held[0], ((c_at + shift) % n_ctx) * piece, piece, 1), shift
        )
        gain_total = came if gain_total is None else gain_total + came

    def both_cores(mine):
        mine = reorder(mine)
        other = twin(mine)
        first = jnp.where(t_at == 0, mine, other)
        second = jnp.where(t_at == 0, other, mine)
        return jnp.concatenate([first, second], 0)[None]

    factor = jnp.sqrt(clip_limit / jnp.maximum(clip_limit, head_peak))
    column_factor = jnp.repeat(factor, HEAD_DIM)
    clipped_query = w_query.astype(f32) * column_factor[None, :]
    clipped_key = w_key.astype(f32) * column_factor[None, :]
    return (
        both_cores(block_out_mine),
        both_cores(input_grad_mine),
        gain_total[0],
        query_out,
        key_out,
        value_out,
        out_proj_out,
        gain_total[1],
        gate_out,
        up_out,
        down_out,
        head_peak,
        clipped_query,
        clipped_key,
    )


def swap_small(gains, along, c_at, n_ctx):
    piece = gains.shape[1]
    placed = jnp.zeros((gains.shape[0], piece * n_ctx), gains.dtype)
    for shift in range(n_ctx):
        placed = lax.dynamic_update_slice_in_dim(
            placed, along(gains, shift), ((c_at - shift) % n_ctx) * piece, 1
        )
    return placed


def gather_plane_small(gains, across, n_bits):
    for step in range(n_bits):
        gains = jnp.concatenate([gains, across(gains, 1 << step)], 1)
    return gains


def solution(mesh):
    placed = (
        P("fsdp", "ctx", None),
        P("fsdp", None),
        P(("fsdp", "ctx")),
        P(("fsdp", "ctx"), "tp"),
        P(("fsdp", "ctx"), "tp"),
        P(("fsdp", "ctx"), "tp"),
        P("tp", ("fsdp", "ctx")),
        P(("fsdp", "ctx")),
        P(("fsdp", "ctx"), "tp"),
        P(("fsdp", "ctx"), "tp"),
        P("tp", ("fsdp", "ctx")),
        P("tp"),
        P("fsdp", "ctx", None),
    )
    return jax.shard_map(
        on_device,
        mesh=mesh,
        in_specs=placed,
        out_specs=(
            P("fsdp", "ctx", None),
            P("fsdp", "ctx", None),
            P(("fsdp", "ctx")),
            P(("fsdp", "ctx"), "tp"),
            P(("fsdp", "ctx"), "tp"),
            P(("fsdp", "ctx"), "tp"),
            P("tp", ("fsdp", "ctx")),
            P(("fsdp", "ctx")),
            P(("fsdp", "ctx"), "tp"),
            P(("fsdp", "ctx"), "tp"),
            P("tp", ("fsdp", "ctx")),
            P("tp"),
            P(("fsdp", "ctx"), "tp"),
            P(("fsdp", "ctx"), "tp"),
        ),
        check_vma=False,
    )
```

```python
import functools

import jax
import jax.numpy as jnp
from jax import lax
from jax.experimental import pallas as pl
from jax.experimental.pallas import tpu as pltpu
from jax.sharding import PartitionSpec as P

HEAD_DIM = 64
NORM_EPS = 1e-05
ROPE_BASE = 130000.0

f32 = jnp.float32
bf16 = jnp.bfloat16

PAIR = 2 * HEAD_DIM
ROWS = 256
VMEM_LIMIT = 48 * 1024 * 1024


def rope_tables(positions):
    half_dim = HEAD_DIM // 2
    step_index = jnp.arange(half_dim, dtype=f32)
    frequency = jnp.power(ROPE_BASE, -2.0 * step_index / (2 * half_dim))
    angles = positions.astype(f32)[:, None] * frequency[None, :]
    cosine, sine = jnp.cos(angles), jnp.sin(angles)
    return (
        jnp.concatenate([cosine, cosine, cosine, cosine], 1),
        jnp.concatenate([-sine, sine, -sine, sine], 1),
    )


def dot(left, right):
    return jnp.dot(left, right, preferred_element_type=f32)


def dot_lt(left, right):
    return lax.dot_general(left, right, (((0,), (0,)), ((), ())), preferred_element_type=f32)


def dot_rt(left, right):
    return lax.dot_general(left, right, (((1,), (1,)), ((), ())), preferred_element_type=f32)


def turn(pair, cosine, sine):
    lane = lax.broadcasted_iota(jnp.int32, pair.shape, 1)
    half_dim = HEAD_DIM // 2
    swapped = jnp.where(
        lane % HEAD_DIM < half_dim,
        pltpu.roll(pair, PAIR - half_dim, 1),
        pltpu.roll(pair, half_dim, 1),
    )
    return pair * cosine + swapped * sine


def project_kernel(pieces, heads_width, x_ref, gain_ref, cosine_ref, sine_ref, *refs):
    weights, normed_ref, out_ref = refs[:pieces], refs[pieces], refs[pieces + 1]
    inputs = x_ref[...].astype(f32)
    inverse = lax.rsqrt(jnp.mean(inputs * inputs, -1, keepdims=True) + NORM_EPS)
    normed = (inputs * inverse * gain_ref[...]).astype(bf16)
    normed_ref[...] = normed
    block = normed.shape[1] // pieces
    proj = None
    for at, weight in enumerate(weights):
        term = dot(normed[:, at * block : (at + 1) * block], weight[:, : 3 * heads_width])
        proj = term if proj is None else proj + term
    cosine, sine = cosine_ref[...], sine_ref[...]
    for at in range(3 * heads_width // PAIR):
        pair = proj[:, at * PAIR : (at + 1) * PAIR]
        if at < 2 * heads_width // PAIR:
            pair = turn(pair, cosine, sine)
        out_ref[:, at * PAIR : (at + 1) * PAIR] = pair.astype(bf16)


def project(tokens, gain, cosine, sine, weights, heads_width, row_block):
    length, width = tokens.shape
    rows = lambda columns: pl.BlockSpec((row_block, columns), lambda i: (i, 0))
    whole = lambda tensor: pl.BlockSpec(tensor.shape, lambda i: (0, 0))
    return pl.pallas_call(
        functools.partial(project_kernel, len(weights), heads_width),
        grid=(length // row_block,),
        out_shape=(
            jax.ShapeDtypeStruct((length, width), bf16),
            jax.ShapeDtypeStruct((length, 3 * heads_width), bf16),
        ),
        in_specs=[rows(width), whole(gain), rows(PAIR), rows(PAIR)] + [whole(w) for w in weights],
        out_specs=(rows(width), rows(3 * heads_width)),
        compiler_params=pltpu.CompilerParams(vmem_limit_bytes=VMEM_LIMIT),
        cost_estimate=pl.CostEstimate(
            flops=6 * length * width * heads_width,
            bytes_accessed=4 * length * width + 8 * width * heads_width,
            transcendentals=length,
        ),
        name="project",
    )(tokens, gain, cosine, sine, *weights)


def sort_spans(order_ref, source, sorted_ref):
    span = sorted_ref.shape[0] // order_ref.shape[0]
    for at in range(order_ref.shape[0]):
        start = pl.multiple_of(order_ref[at] * span, span)
        sorted_ref[pl.ds(start, span), :] = source[at * span : (at + 1) * span, :]


def unsorted_span(order_ref, sorted_ref, at):
    span = sorted_ref.shape[0] // order_ref.shape[0]
    start = pl.multiple_of(order_ref[at] * span, span)
    return sorted_ref[pl.ds(start, span), :]


def causal(scores, first_row):
    row = lax.broadcasted_iota(jnp.int32, scores.shape, 0) + first_row
    column = lax.broadcasted_iota(jnp.int32, scores.shape, 1)
    return jnp.where(column <= row, scores, -1e30)


def forward_kernel(order_ref, q_ref, k_ref, v_ref, out_ref, log_ref, peak_ref, q_s, k_s, v_s, o_s):
    length = q_ref.shape[0]
    block = min(ROWS, length)
    scale = HEAD_DIM ** (-0.5)
    for source, held in ((q_ref, q_s), (k_ref, k_s), (v_ref, v_s)):
        sort_spans(order_ref, source, held)
    lane = lax.broadcasted_iota(jnp.int32, (block, PAIR), 1)
    peaks = [None, None]
    for start in range(0, length, block):
        end = start + block
        query, key, value = q_s[start:end, :], k_s[:end, :], v_s[:end, :]
        attended, logs = [], []
        for head in range(2):
            mine = (lane // HEAD_DIM) == head
            scores = causal(dot_rt(jnp.where(mine, query, 0), key) * scale, start)
            row_max = jnp.max(scores, 1, keepdims=True)
            terms = jnp.exp(scores - row_max)
            total = jnp.sum(terms, 1, keepdims=True)
            attended.append(dot((terms * (1.0 / total)).astype(bf16), value))
            logs.append(row_max + jnp.log(total))
            top = jnp.max(row_max)
            peaks[head] = top if peaks[head] is None else jnp.maximum(peaks[head], top)
        o_s[start:end, :] = jnp.where(lane < HEAD_DIM, attended[0], attended[1])
        log_ref[0, start:end, :] = jnp.where(lane < HEAD_DIM, logs[0], logs[1])
    for at in range(order_ref.shape[0]):
        span = length // order_ref.shape[0]
        out_ref[at * span : (at + 1) * span, :] = unsorted_span(order_ref, o_s, at).astype(bf16)
    lane = lax.broadcasted_iota(jnp.int32, peak_ref.shape, 2)
    peak_ref[...] = jnp.where(lane < HEAD_DIM, peaks[0], peaks[1])


def attend(order, qkv):
    length = qkv.shape[0]
    pairs = qkv.shape[1] // (3 * PAIR)
    column = lambda first: pl.BlockSpec((length, PAIR), lambda g, order: (0, first + g))
    return pl.pallas_call(
        forward_kernel,
        grid_spec=pltpu.PrefetchScalarGridSpec(
            num_scalar_prefetch=1,
            grid=(pairs,),
            in_specs=[column(0), column(pairs), column(2 * pairs)],
            out_specs=(
                column(0),
                pl.BlockSpec((1, length, PAIR), lambda g, order: (g, 0, 0)),
                pl.BlockSpec((1, 8, PAIR), lambda g, order: (g, 0, 0)),
            ),
            scratch_shapes=[pltpu.VMEM((length, PAIR), bf16)] * 3 + [pltpu.VMEM((length, PAIR), f32)],
        ),
        out_shape=(
            jax.ShapeDtypeStruct((length, pairs * PAIR), bf16),
            jax.ShapeDtypeStruct((pairs, length, PAIR), f32),
            jax.ShapeDtypeStruct((pairs, 8, PAIR), f32),
        ),
        compiler_params=pltpu.CompilerParams(vmem_limit_bytes=VMEM_LIMIT),
        cost_estimate=pl.CostEstimate(
            flops=16 * pairs * length * length * PAIR,
            bytes_accessed=8 * pairs * length * PAIR,
            transcendentals=2 * pairs * length * length,
        ),
        name="attend",
    )(order, qkv, qkv, qkv)


def backward_kernel(
    order_ref, q_ref, k_ref, v_ref, g_ref, log_ref, cosine_ref, sine_ref, out_ref, *held
):
    q_s, k_s, v_s, g_s, dq_s, dk_s, dv_s = held
    length = q_ref.shape[0]
    block = min(ROWS, length)
    scale = HEAD_DIM ** (-0.5)
    for source, into in ((q_ref, q_s), (k_ref, k_s), (v_ref, v_s), (g_ref, g_s)):
        sort_spans(order_ref, source, into)
    dk_s[...] = jnp.zeros_like(dk_s)
    dv_s[...] = jnp.zeros_like(dv_s)
    lane = lax.broadcasted_iota(jnp.int32, (block, PAIR), 1)
    for start in range(0, length, block):
        end = start + block
        query, grad = q_s[start:end, :], g_s[start:end, :]
        key, value = k_s[:end, :], v_s[:end, :]
        grad_query = []
        for head in range(2):
            mine = (lane // HEAD_DIM) == head
            query_h = jnp.where(mine, query, 0)
            grad_h = jnp.where(mine, grad, 0)
            log_h = log_ref[0, start:end, head * HEAD_DIM : head * HEAD_DIM + 1]
            scores = causal(dot_rt(query_h, key) * scale, start)
            prob = jnp.exp(scores - log_h)
            grad_prob = dot_rt(grad_h, value)
            delta = jnp.sum(prob * grad_prob, 1, keepdims=True)
            grad_score = (prob * (grad_prob - delta)).astype(bf16)
            grad_query.append(dot(grad_score, key))
            dk_s[:end, :] += dot_lt(grad_score, query_h)
            dv_s[:end, :] += dot_lt(prob.astype(bf16), grad_h)
        dq_s[start:end, :] = jnp.where(lane < HEAD_DIM, grad_query[0], grad_query[1])
    pairs = out_ref.shape[1] // (3 * PAIR)
    column = pl.program_id(0)
    span = length // order_ref.shape[0]
    for at in range(order_ref.shape[0]):
        rows = slice(at * span, (at + 1) * span)
        cosine, sine = cosine_ref[rows, :], sine_ref[rows, :]
        for which, source in enumerate((dq_s, dk_s, dv_s)):
            part = unsorted_span(order_ref, source, at)
            if which < 2:
                part = turn(part * scale, cosine, -sine)
            start = pl.multiple_of((which * pairs + column) * PAIR, PAIR)
            out_ref[rows, pl.ds(start, PAIR)] = part.astype(bf16)


def attend_back(order, qkv, grad, logs, cosine, sine):
    length = qkv.shape[0]
    pairs = qkv.shape[1] // (3 * PAIR)
    column = lambda first: pl.BlockSpec((length, PAIR), lambda g, order: (0, first + g))
    whole = pl.BlockSpec((length, PAIR), lambda g, order: (0, 0))
    return pl.pallas_call(
        backward_kernel,
        grid_spec=pltpu.PrefetchScalarGridSpec(
            num_scalar_prefetch=1,
            grid=(pairs,),
            in_specs=[
                column(0),
                column(pairs),
                column(2 * pairs),
                column(0),
                pl.BlockSpec((1, length, PAIR), lambda g, order: (g, 0, 0)),
                whole,
                whole,
            ],
            out_specs=pl.BlockSpec((length, 3 * pairs * PAIR), lambda g, order: (0, 0)),
            scratch_shapes=[pltpu.VMEM((length, PAIR), bf16)] * 4
            + [pltpu.VMEM((length, PAIR), f32)] * 3,
        ),
        out_shape=jax.ShapeDtypeStruct(qkv.shape, bf16),
        compiler_params=pltpu.CompilerParams(vmem_limit_bytes=VMEM_LIMIT),
        cost_estimate=pl.CostEstimate(
            flops=40 * pairs * length * length * PAIR,
            bytes_accessed=16 * pairs * length * PAIR,
            transcendentals=2 * pairs * length * length,
        ),
        name="attend_back",
    )(order, qkv, qkv, qkv, grad, logs, cosine, sine)


def on_device(
    block_in,
    span_order,
    attn_gain,
    w_query,
    w_key,
    w_value,
    w_out,
    mlp_gain,
    w_gate,
    w_up,
    w_down,
    clip_limit,
    cotangent,
):
    n_ctx = lax.axis_size("ctx")
    n_fsdp = lax.axis_size("fsdp")
    n_bits = n_fsdp.bit_length() - 1
    c_at = lax.axis_index("ctx")
    f_at = lax.axis_index("fsdp")
    t_at = lax.axis_index("tp")
    row_count, width = block_in.shape[1:]
    span_len = row_count // 2
    feature_block = width // n_fsdp

    def along(tensor, shift):
        if shift % n_ctx == 0:
            return tensor
        return lax.ppermute(tensor, "ctx", [(i, (i + shift) % n_ctx) for i in range(n_ctx)])

    def across(tensor, mask):
        return lax.ppermute(tensor, "fsdp", [(i, i ^ mask) for i in range(n_fsdp)])

    def twin(tensor):
        return lax.ppermute(tensor, "tp", [(0, 1), (1, 0)])

    def after(tensor, *earlier):
        return lax.optimization_barrier((tensor, *earlier))[0]

    def reorder(tensor):
        return jnp.concatenate(
            [
                lax.dynamic_slice_in_dim(tensor, (f_at ^ m) * feature_block, feature_block, -1)
                for m in range(n_fsdp)
            ],
            -1,
        )

    def swap_ctx(tensor):
        piece = tensor.shape[0] // n_ctx
        columns = tensor.shape[1]
        placed = jnp.zeros((piece, n_ctx * columns), f32)
        for shift in range(n_ctx):
            sent = lax.dynamic_slice_in_dim(tensor, ((c_at + shift) % n_ctx) * piece, piece, 0)
            placed = lax.dynamic_update_slice_in_dim(
                placed, along(sent, shift).astype(f32), ((c_at - shift) % n_ctx) * columns, 1
            )
        return placed

    def swap_columns(*tensors):
        rows, columns = tensors[0].shape
        piece = columns // n_ctx
        width_here = piece * len(tensors)
        placed = jnp.zeros((n_ctx, rows, width_here), tensors[0].dtype)
        for shift in range(n_ctx):
            start = ((c_at + shift) % n_ctx) * piece
            sent = jnp.concatenate(
                [lax.dynamic_slice_in_dim(tensor, start, piece, 1) for tensor in tensors], 1
            )
            placed = lax.dynamic_update_slice_in_dim(
                placed, along(sent, shift)[None], (c_at - shift) % n_ctx, 0
            )
        return placed.reshape(n_ctx * rows, width_here)

    def swap_side(tensor, count, turn_last):
        piece = tensor.shape[0] // n_ctx
        columns = tensor.shape[1] // count
        placed = [jnp.zeros((piece, n_ctx * columns), f32)] * count
        if turn_last:
            placed[-1] = placed[-1].T
        for shift in range(n_ctx):
            sent = lax.dynamic_slice_in_dim(tensor, ((c_at + shift) % n_ctx) * piece, piece, 0)
            came = along(sent, shift)
            start = ((c_at - shift) % n_ctx) * columns
            for at in range(count):
                part = came[:, at * columns : (at + 1) * columns].astype(f32)
                turned_here = turn_last and at == count - 1
                placed[at] = lax.dynamic_update_slice_in_dim(
                    placed[at], part.T if turned_here else part, start, 0 if turned_here else 1
                )
        return placed

    def plane_pieces(tensor):
        return [tensor] + [across(tensor, m) for m in range(1, n_fsdp)]

    def gather_plane(tensor):
        return jnp.concatenate(plane_pieces(tensor), 0)

    def scatter_plane(*tensors, late=()):
        size = tensors[0].shape[0] // n_fsdp
        total = jnp.concatenate([tensor[:size] for tensor in tensors], 1)
        for m in range(1, n_fsdp):
            sent = jnp.concatenate(
                [tensor[m * size : (m + 1) * size].astype(bf16) for tensor in tensors], 1
            )
            total = total + after(across(sent, m), *late).astype(f32)
        return total.astype(bf16)

    def gather_tokens(own):
        return lax.all_gather(own, ("ctx", "tp"), axis=0, tiled=True)

    def scatter_tokens(partial):
        return lax.psum_scatter(
            partial.astype(bf16), ("ctx", "tp"), scatter_dimension=0, tiled=True
        ).astype(f32)

    order_row = span_order[0]
    positions = (
        order_row[:, None] * span_len + jnp.arange(span_len, dtype=jnp.int32)[None, :]
    ).reshape(-1)
    cosine, sine = rope_tables(positions)
    length = positions.shape[0]

    def own_rows(tensor):
        return reorder(lax.dynamic_slice_in_dim(tensor[0], t_at * span_len, span_len, 0))

    inputs_own = own_rows(block_in)
    cot_own = own_rows(cotangent)

    gains = jnp.stack([attn_gain, mlp_gain])
    gains = gather_plane_small(swap_small(gains, along, c_at, n_ctx), across, n_bits)
    gain_one, gain_two = gains[0].astype(f32), gains[1].astype(f32)

    heads_width = w_query.shape[1] // n_ctx
    attn_part = swap_columns(w_query, w_key, w_value, w_out.T)
    inputs_low = gather_tokens(after(inputs_own, attn_part))
    attn_pieces = plane_pieces(attn_part)
    attn_full = jnp.concatenate(attn_pieces, 0)
    gate_part = swap_columns(after(w_gate, inputs_low))
    late_part = swap_columns(after(w_up, gate_part), w_down.T)
    gate_full = gather_plane(gate_part)
    hidden_here = gate_full.shape[1]
    up_full = gather_plane(after(late_part, gate_full)[:, :hidden_here])
    down_full = gather_plane(after(late_part, up_full)[:, hidden_here:])
    qkv_full = attn_full[:, : 3 * heads_width]
    out_full = attn_full[:, 3 * heads_width :]

    heads_here = heads_width // HEAD_DIM
    normed_one, qkv = project(
        inputs_low, gain_one[None], cosine, sine, attn_pieces, heads_width, row_count
    )
    qkv = after(qkv, gate_part)
    attn_low, log_total, peaks = attend(order_row, qkv)
    head_max = peaks[:, 0, ::HEAD_DIM].reshape(-1)
    attn_low = after(attn_low, late_part, gate_full)
    attn_sum = scatter_tokens(dot_rt(attn_low, out_full))
    attn_sum = after(attn_sum, up_full)

    peak = head_max
    for step in range(n_bits):
        peak = jnp.maximum(peak, across(peak, 1 << step))
    head_peak = jnp.zeros((n_ctx * heads_here,), f32)
    for shift in range(n_ctx):
        head_peak = lax.dynamic_update_slice_in_dim(
            head_peak, along(peak, shift), ((c_at - shift) % n_ctx) * heads_here, 0
        )

    inputs_mine = inputs_own.astype(f32)
    resid = inputs_mine + attn_sum
    inv_two = lax.rsqrt(jnp.mean(resid * resid, -1, keepdims=True) + NORM_EPS)
    scaled_two = resid * inv_two
    normed_two = gather_tokens((scaled_two * gain_two).astype(bf16))
    cot_all = gather_tokens(after(cot_own, normed_two))
    gate_act = dot(normed_two, gate_full)
    up_act = dot(normed_two, up_full)
    sig_gate = jax.nn.sigmoid(gate_act)
    silu_gate = gate_act * sig_gate
    hidden = (silu_gate * up_act).astype(bf16)
    grad_hidden = dot(cot_all, down_full)
    silu_slope = sig_gate * (1.0 + gate_act * (1.0 - sig_gate))
    grad_gate = (grad_hidden * up_act * silu_slope).astype(bf16)
    grad_up = (grad_hidden * silu_gate).astype(bf16)
    back_two = (dot_rt(grad_gate, gate_full) + dot_rt(grad_up, up_full)).astype(bf16)
    grad_normed_two = scatter_tokens(back_two)
    hidden_late, gate_late, up_late = (after(g, back_two) for g in (hidden, grad_gate, grad_up))
    grad_w_down = dot_lt(cot_all, hidden_late)
    grad_w_gate = dot_lt(normed_two, gate_late)
    grad_w_up = dot_lt(normed_two, up_late)
    mlp_partial = dot_rt(hidden_late, down_full).astype(bf16)
    grad_normed_two = after(grad_normed_two, grad_w_down, grad_w_gate, grad_w_up, mlp_partial)

    grad_gain_two = jnp.sum(grad_normed_two * scaled_two, axis=0)
    weighted_two = grad_normed_two * gain_two
    grad_resid = cot_own.astype(f32) + inv_two * (
        weighted_two - scaled_two * jnp.mean(weighted_two * scaled_two, -1, keepdims=True)
    )
    grad_low = gather_tokens(grad_resid.astype(bf16))
    down_sum = scatter_plane(grad_w_down, late=(grad_normed_two,))
    grad_low = after(grad_low, down_sum)
    mlp_sum = scatter_tokens(after(mlp_partial, grad_low))
    block_out_mine = (resid + mlp_sum).astype(bf16)

    grad_attended = dot(grad_low, out_full).astype(bf16)
    down_out = swap_ctx(after(down_sum, grad_low)).T
    late_sum = scatter_plane(after(grad_w_gate, down_sum), grad_w_up, late=(grad_attended,))

    grad_proj = attend_back(order_row, qkv, grad_attended, log_total, cosine, sine)
    grad_proj = after(grad_proj, late_sum, down_out)
    back_one = dot_rt(grad_proj, qkv_full).astype(bf16)
    grad_normed_one = scatter_tokens(back_one)
    proj_late = after(grad_proj, back_one)
    attn_sum_grad = scatter_plane(dot_lt(normed_one, proj_late), dot_lt(grad_low, attn_low))
    gate_out, up_out = swap_side(after(late_sum, back_one), 2, False)
    query_out, key_out, value_out, out_proj_out = swap_side(after(attn_sum_grad, up_out), 4, True)
    inputs = inputs_low.astype(f32)
    inv_one = lax.rsqrt(jnp.mean(inputs * inputs, -1, keepdims=True) + NORM_EPS)
    grad_gain_one = jnp.sum(back_one.astype(f32) * (inputs * inv_one), axis=0)

    inv_mine = lax.rsqrt(jnp.mean(inputs_mine * inputs_mine, -1, keepdims=True) + NORM_EPS)
    scaled_one = inputs_mine * inv_mine
    weighted_one = grad_normed_one * gain_one
    input_grad_mine = grad_resid + inv_mine * (
        weighted_one - scaled_one * jnp.mean(weighted_one * scaled_one, -1, keepdims=True)
    )

    gain_grads = jnp.stack([grad_gain_one, grad_gain_two])
    gain_grads = gain_grads + twin(gain_grads)
    held = {m: gain_grads[:, m * feature_block : (m + 1) * feature_block] for m in range(n_fsdp)}
    for bit in [1 << step for step in range(n_bits)]:
        kept = [m for m in sorted(held) if not m & bit]
        came = across(jnp.concatenate([held[m | bit] for m in kept], 1), bit)
        held = {
            m: held[m] + came[:, at * feature_block : (at + 1) * feature_block]
            for at, m in enumerate(kept)
        }
    piece = feature_block // n_ctx
    gain_total = None
    for shift in range(n_ctx):
        came = along(
            lax.dynamic_slice_in_dim(held[0], ((c_at + shift) % n_ctx) * piece, piece, 1), shift
        )
        gain_total = came if gain_total is None else gain_total + came

    def both_cores(mine):
        mine = reorder(mine)
        other = twin(mine)
        first = jnp.where(t_at == 0, mine, other)
        second = jnp.where(t_at == 0, other, mine)
        return jnp.concatenate([first, second], 0)[None]

    factor = jnp.sqrt(clip_limit / jnp.maximum(clip_limit, head_peak))
    column_factor = jnp.repeat(factor, HEAD_DIM)
    clipped_query = w_query.astype(f32) * column_factor[None, :]
    clipped_key = w_key.astype(f32) * column_factor[None, :]
    return (
        both_cores(block_out_mine),
        both_cores(input_grad_mine),
        gain_total[0],
        query_out,
        key_out,
        value_out,
        out_proj_out,
        gain_total[1],
        gate_out,
        up_out,
        down_out,
        head_peak,
        clipped_query,
        clipped_key,
    )


def swap_small(gains, along, c_at, n_ctx):
    piece = gains.shape[1]
    placed = jnp.zeros((gains.shape[0], piece * n_ctx), gains.dtype)
    for shift in range(n_ctx):
        placed = lax.dynamic_update_slice_in_dim(
            placed, along(gains, shift), ((c_at - shift) % n_ctx) * piece, 1
        )
    return placed


def gather_plane_small(gains, across, n_bits):
    for step in range(n_bits):
        gains = jnp.concatenate([gains, across(gains, 1 << step)], 1)
    return gains


def solution(mesh):
    placed = (
        P("fsdp", "ctx", None),
        P("fsdp", None),
        P(("fsdp", "ctx")),
        P(("fsdp", "ctx"), "tp"),
        P(("fsdp", "ctx"), "tp"),
        P(("fsdp", "ctx"), "tp"),
        P("tp", ("fsdp", "ctx")),
        P(("fsdp", "ctx")),
        P(("fsdp", "ctx"), "tp"),
        P(("fsdp", "ctx"), "tp"),
        P("tp", ("fsdp", "ctx")),
        P("tp"),
        P("fsdp", "ctx", None),
    )
    return jax.shard_map(
        on_device,
        mesh=mesh,
        in_specs=placed,
        out_specs=(
            P("fsdp", "ctx", None),
            P("fsdp", "ctx", None),
            P(("fsdp", "ctx")),
            P(("fsdp", "ctx"), "tp"),
            P(("fsdp", "ctx"), "tp"),
            P(("fsdp", "ctx"), "tp"),
            P("tp", ("fsdp", "ctx")),
            P(("fsdp", "ctx")),
            P(("fsdp", "ctx"), "tp"),
            P(("fsdp", "ctx"), "tp"),
            P("tp", ("fsdp", "ctx")),
            P("tp"),
            P(("fsdp", "ctx"), "tp"),
            P(("fsdp", "ctx"), "tp"),
        ),
        check_vma=False,
    )
```

```python
import functools

import jax
import jax.numpy as jnp
from jax import lax
from jax.experimental import pallas as pl
from jax.experimental.pallas import tpu as pltpu
from jax.sharding import PartitionSpec as P

HEAD_DIM = 64
NORM_EPS = 1e-05
ROPE_BASE = 130000.0

f32 = jnp.float32
bf16 = jnp.bfloat16

PAIR = 2 * HEAD_DIM
ROWS = 256
VMEM_LIMIT = 48 * 1024 * 1024


def rope_tables(positions):
    half_dim = HEAD_DIM // 2
    step_index = jnp.arange(half_dim, dtype=f32)
    frequency = jnp.power(ROPE_BASE, -2.0 * step_index / (2 * half_dim))
    angles = positions.astype(f32)[:, None] * frequency[None, :]
    cosine, sine = jnp.cos(angles), jnp.sin(angles)
    return (
        jnp.concatenate([cosine, cosine, cosine, cosine], 1),
        jnp.concatenate([-sine, sine, -sine, sine], 1),
    )


def dot(left, right):
    return jnp.dot(left, right, preferred_element_type=f32)


def dot_lt(left, right):
    return lax.dot_general(left, right, (((0,), (0,)), ((), ())), preferred_element_type=f32)


def dot_rt(left, right):
    return lax.dot_general(left, right, (((1,), (1,)), ((), ())), preferred_element_type=f32)


def place_kernel(count, ways, at_ref, *refs):
    pieces = len(refs) - count
    slot = lax.rem(at_ref[0] + pieces - pl.program_id(0), pieces)
    for at in range(pieces):

        @pl.when(slot == at)
        def _(source=refs[at]):
            columns = source.shape[1] // count
            for which in range(count):
                part = source[:, which * columns : (which + 1) * columns]
                target = refs[pieces + which]
                part = part.astype(target.dtype)
                target[...] = part.T if ways[which] == "turned" else part


def place(at, pieces, count, ways, dtype):
    slots = len(pieces)
    rows, columns = pieces[0].shape
    columns = columns // count
    shapes = {
        "down": ((slots * rows, columns), (rows, columns), lambda b, at: (b, 0)),
        "side": ((rows, slots * columns), (rows, columns), lambda b, at: (0, b)),
        "turned": ((slots * columns, rows), (columns, rows), lambda b, at: (b, 0)),
    }
    return pl.pallas_call(
        functools.partial(place_kernel, count, ways),
        grid_spec=pltpu.PrefetchScalarGridSpec(
            num_scalar_prefetch=1,
            grid=(slots,),
            in_specs=[pl.BlockSpec(piece.shape, lambda b, at: (0, 0)) for piece in pieces],
            out_specs=[pl.BlockSpec(shapes[way][1], shapes[way][2]) for way in ways],
        ),
        out_shape=[jax.ShapeDtypeStruct(shapes[way][0], dtype) for way in ways],
        compiler_params=pltpu.CompilerParams(vmem_limit_bytes=VMEM_LIMIT),
        cost_estimate=pl.CostEstimate(
            flops=0, bytes_accessed=6 * slots * rows * columns * count, transcendentals=0
        ),
        name="place",
    )(at.astype(jnp.int32)[None], *pieces)


def turn(pair, cosine, sine):
    lane = lax.broadcasted_iota(jnp.int32, pair.shape, 1)
    half_dim = HEAD_DIM // 2
    swapped = jnp.where(
        lane % HEAD_DIM < half_dim,
        pltpu.roll(pair, PAIR - half_dim, 1),
        pltpu.roll(pair, half_dim, 1),
    )
    return pair * cosine + swapped * sine


def project_kernel(pieces, heads_width, x_ref, gain_ref, cosine_ref, sine_ref, *refs):
    weights, normed_ref, out_ref = refs[:pieces], refs[pieces], refs[pieces + 1]
    inputs = x_ref[...].astype(f32)
    inverse = lax.rsqrt(jnp.mean(inputs * inputs, -1, keepdims=True) + NORM_EPS)
    normed = (inputs * inverse * gain_ref[...]).astype(bf16)
    normed_ref[...] = normed
    block = normed.shape[1] // pieces
    proj = None
    for at, weight in enumerate(weights):
        term = dot(normed[:, at * block : (at + 1) * block], weight[:, : 3 * heads_width])
        proj = term if proj is None else proj + term
    cosine, sine = cosine_ref[...], sine_ref[...]
    for at in range(3 * heads_width // PAIR):
        pair = proj[:, at * PAIR : (at + 1) * PAIR]
        if at < 2 * heads_width // PAIR:
            pair = turn(pair, cosine, sine)
        out_ref[:, at * PAIR : (at + 1) * PAIR] = pair.astype(bf16)


def project(tokens, gain, cosine, sine, weights, heads_width, row_block):
    length, width = tokens.shape
    rows = lambda columns: pl.BlockSpec((row_block, columns), lambda i: (i, 0))
    whole = lambda tensor: pl.BlockSpec(tensor.shape, lambda i: (0, 0))
    return pl.pallas_call(
        functools.partial(project_kernel, len(weights), heads_width),
        grid=(length // row_block,),
        out_shape=(
            jax.ShapeDtypeStruct((length, width), bf16),
            jax.ShapeDtypeStruct((length, 3 * heads_width), bf16),
        ),
        in_specs=[rows(width), whole(gain), rows(PAIR), rows(PAIR)] + [whole(w) for w in weights],
        out_specs=(rows(width), rows(3 * heads_width)),
        compiler_params=pltpu.CompilerParams(vmem_limit_bytes=VMEM_LIMIT),
        cost_estimate=pl.CostEstimate(
            flops=length * width * heads_width,
            bytes_accessed=4 * length * width + 8 * width * heads_width,
            transcendentals=length,
        ),
        name="project",
    )(tokens, gain, cosine, sine, *weights)


def sort_spans(order_ref, source, sorted_ref):
    span = sorted_ref.shape[0] // order_ref.shape[0]
    for at in range(order_ref.shape[0]):
        start = pl.multiple_of(order_ref[at] * span, span)
        sorted_ref[pl.ds(start, span), :] = source[at * span : (at + 1) * span, :]


def unsorted_span(order_ref, sorted_ref, at):
    span = sorted_ref.shape[0] // order_ref.shape[0]
    start = pl.multiple_of(order_ref[at] * span, span)
    return sorted_ref[pl.ds(start, span), :]


def causal(scores, first_row):
    row = lax.broadcasted_iota(jnp.int32, scores.shape, 0) + first_row
    column = lax.broadcasted_iota(jnp.int32, scores.shape, 1)
    return jnp.where(column <= row, scores, -1e30)


def forward_kernel(order_ref, q_ref, k_ref, v_ref, out_ref, log_ref, peak_ref, q_s, k_s, v_s, o_s):
    length = q_ref.shape[0]
    block = min(ROWS, length)
    scale = HEAD_DIM ** (-0.5)
    for source, held in ((q_ref, q_s), (k_ref, k_s), (v_ref, v_s)):
        sort_spans(order_ref, source, held)
    lane = lax.broadcasted_iota(jnp.int32, (block, PAIR), 1)
    peaks = [None, None]
    for start in range(0, length, block):
        end = start + block
        query, key, value = q_s[start:end, :], k_s[:end, :], v_s[:end, :]
        attended, logs = [], []
        for head in range(2):
            mine = (lane // HEAD_DIM) == head
            scores = causal(dot_rt(jnp.where(mine, query, 0), key) * scale, start)
            row_max = jnp.max(scores, 1, keepdims=True)
            terms = jnp.exp(scores - row_max)
            total = jnp.sum(terms, 1, keepdims=True)
            attended.append(dot((terms * (1.0 / total)).astype(bf16), value))
            logs.append(row_max + jnp.log(total))
            top = jnp.max(row_max)
            peaks[head] = top if peaks[head] is None else jnp.maximum(peaks[head], top)
        o_s[start:end, :] = jnp.where(lane < HEAD_DIM, attended[0], attended[1])
        log_ref[0, start:end, :] = jnp.where(lane < HEAD_DIM, logs[0], logs[1])
    for at in range(order_ref.shape[0]):
        span = length // order_ref.shape[0]
        out_ref[at * span : (at + 1) * span, :] = unsorted_span(order_ref, o_s, at).astype(bf16)
    lane = lax.broadcasted_iota(jnp.int32, peak_ref.shape, 2)
    peak_ref[...] = jnp.where(lane < HEAD_DIM, peaks[0], peaks[1])


def attend(order, qkv):
    length = qkv.shape[0]
    pairs = qkv.shape[1] // (3 * PAIR)
    column = lambda first: pl.BlockSpec((length, PAIR), lambda g, order: (0, first + g))
    return pl.pallas_call(
        forward_kernel,
        grid_spec=pltpu.PrefetchScalarGridSpec(
            num_scalar_prefetch=1,
            grid=(pairs,),
            in_specs=[column(0), column(pairs), column(2 * pairs)],
            out_specs=(
                column(0),
                pl.BlockSpec((1, length, PAIR), lambda g, order: (g, 0, 0)),
                pl.BlockSpec((1, 8, PAIR), lambda g, order: (g, 0, 0)),
            ),
            scratch_shapes=[pltpu.VMEM((length, PAIR), bf16)] * 3 + [pltpu.VMEM((length, PAIR), f32)],
        ),
        out_shape=(
            jax.ShapeDtypeStruct((length, pairs * PAIR), bf16),
            jax.ShapeDtypeStruct((pairs, length, PAIR), f32),
            jax.ShapeDtypeStruct((pairs, 8, PAIR), f32),
        ),
        compiler_params=pltpu.CompilerParams(vmem_limit_bytes=VMEM_LIMIT),
        cost_estimate=pl.CostEstimate(
            flops=2 * pairs * length * length * PAIR,
            bytes_accessed=8 * pairs * length * PAIR,
            transcendentals=pairs * length,
        ),
        name="attend",
    )(order, qkv, qkv, qkv)


def backward_kernel(
    order_ref, q_ref, k_ref, v_ref, g_ref, log_ref, cosine_ref, sine_ref, out_ref, *held
):
    q_s, k_s, v_s, g_s, dq_s, dk_s, dv_s = held
    length = q_ref.shape[0]
    block = min(ROWS, length)
    scale = HEAD_DIM ** (-0.5)
    for source, into in ((q_ref, q_s), (k_ref, k_s), (v_ref, v_s), (g_ref, g_s)):
        sort_spans(order_ref, source, into)
    dk_s[...] = jnp.zeros_like(dk_s)
    dv_s[...] = jnp.zeros_like(dv_s)
    lane = lax.broadcasted_iota(jnp.int32, (block, PAIR), 1)
    for start in range(0, length, block):
        end = start + block
        query, grad = q_s[start:end, :], g_s[start:end, :]
        key, value = k_s[:end, :], v_s[:end, :]
        grad_query = []
        for head in range(2):
            mine = (lane // HEAD_DIM) == head
            query_h = jnp.where(mine, query, 0)
            grad_h = jnp.where(mine, grad, 0)
            log_h = log_ref[0, start:end, head * HEAD_DIM : head * HEAD_DIM + 1]
            scores = causal(dot_rt(query_h, key) * scale, start)
            prob = jnp.exp(scores - log_h)
            grad_prob = dot_rt(grad_h, value)
            delta = jnp.sum(prob * grad_prob, 1, keepdims=True)
            grad_score = (prob * (grad_prob - delta)).astype(bf16)
            grad_query.append(dot(grad_score, key))
            dk_s[:end, :] += dot_lt(grad_score, query_h)
            dv_s[:end, :] += dot_lt(prob.astype(bf16), grad_h)
        dq_s[start:end, :] = jnp.where(lane < HEAD_DIM, grad_query[0], grad_query[1])
    pairs = out_ref.shape[1] // (3 * PAIR)
    column = pl.program_id(0)
    span = length // order_ref.shape[0]
    for at in range(order_ref.shape[0]):
        rows = slice(at * span, (at + 1) * span)
        cosine, sine = cosine_ref[rows, :], sine_ref[rows, :]
        for which, source in enumerate((dq_s, dk_s, dv_s)):
            part = unsorted_span(order_ref, source, at)
            if which < 2:
                part = turn(part * scale, cosine, -sine)
            start = pl.multiple_of((which * pairs + column) * PAIR, PAIR)
            out_ref[rows, pl.ds(start, PAIR)] = part.astype(bf16)


def attend_back(order, qkv, grad, logs, cosine, sine):
    length = qkv.shape[0]
    pairs = qkv.shape[1] // (3 * PAIR)
    column = lambda first: pl.BlockSpec((length, PAIR), lambda g, order: (0, first + g))
    whole = pl.BlockSpec((length, PAIR), lambda g, order: (0, 0))
    return pl.pallas_call(
        backward_kernel,
        grid_spec=pltpu.PrefetchScalarGridSpec(
            num_scalar_prefetch=1,
            grid=(pairs,),
            in_specs=[
                column(0),
                column(pairs),
                column(2 * pairs),
                column(0),
                pl.BlockSpec((1, length, PAIR), lambda g, order: (g, 0, 0)),
                whole,
                whole,
            ],
            out_specs=pl.BlockSpec((length, 3 * pairs * PAIR), lambda g, order: (0, 0)),
            scratch_shapes=[pltpu.VMEM((length, PAIR), bf16)] * 4
            + [pltpu.VMEM((length, PAIR), f32)] * 3,
        ),
        out_shape=jax.ShapeDtypeStruct(qkv.shape, bf16),
        compiler_params=pltpu.CompilerParams(vmem_limit_bytes=VMEM_LIMIT),
        cost_estimate=pl.CostEstimate(
            flops=2 * pairs * length * length * PAIR,
            bytes_accessed=16 * pairs * length * PAIR,
            transcendentals=pairs * length,
        ),
        name="attend_back",
    )(order, qkv, qkv, qkv, grad, logs, cosine, sine)


def on_device(
    block_in,
    span_order,
    attn_gain,
    w_query,
    w_key,
    w_value,
    w_out,
    mlp_gain,
    w_gate,
    w_up,
    w_down,
    clip_limit,
    cotangent,
):
    n_ctx = lax.axis_size("ctx")
    n_fsdp = lax.axis_size("fsdp")
    n_bits = n_fsdp.bit_length() - 1
    c_at = lax.axis_index("ctx")
    f_at = lax.axis_index("fsdp")
    t_at = lax.axis_index("tp")
    row_count, width = block_in.shape[1:]
    span_len = row_count // 2
    feature_block = width // n_fsdp

    def along(tensor, shift):
        if shift % n_ctx == 0:
            return tensor
        return lax.ppermute(tensor, "ctx", [(i, (i + shift) % n_ctx) for i in range(n_ctx)])

    def across(tensor, mask):
        return lax.ppermute(tensor, "fsdp", [(i, i ^ mask) for i in range(n_fsdp)])

    def twin(tensor):
        return lax.ppermute(tensor, "tp", [(0, 1), (1, 0)])

    def after(tensor, *earlier):
        return lax.optimization_barrier((tensor, *earlier))[0]

    def reorder(tensor):
        return jnp.concatenate(
            [
                lax.dynamic_slice_in_dim(tensor, (f_at ^ m) * feature_block, feature_block, -1)
                for m in range(n_fsdp)
            ],
            -1,
        )

    def swap_columns(*tensors, late=()):
        piece = tensors[0].shape[1] // n_ctx
        came = []
        for shift in range(n_ctx):
            start = ((c_at + shift) % n_ctx) * piece
            sent = [lax.dynamic_slice_in_dim(tensor, start, piece, 1) for tensor in tensors]
            came.append(after(along(jnp.concatenate(sent, 1), shift), *late))
        return place(c_at, came, 1, ("down",), bf16)[0]

    def swap_rows(tensor, ways, late=()):
        piece = tensor.shape[0] // n_ctx
        came = []
        for shift in range(n_ctx):
            sent = lax.dynamic_slice_in_dim(tensor, ((c_at + shift) % n_ctx) * piece, piece, 0)
            came.append(after(along(sent, shift), *late))
        return place(c_at, came, len(ways), ways, f32)

    def plane_pieces(tensor, late=()):
        if n_fsdp != 4:
            return [tensor] + [after(across(tensor, m), *late) for m in range(1, n_fsdp)]
        half = tensor.shape[0] // 2
        near_x, near_y = across(tensor, 1), across(tensor, 2)
        far = [across(near_x[:half], 2), across(near_y[half:], 1)]
        pieces = [tensor, near_x, near_y, jnp.concatenate(far, 0)]
        return [after(piece, *late) for piece in pieces]

    def gather_plane(tensor, late=()):
        return jnp.concatenate(plane_pieces(tensor, late), 0)

    def scatter_plane(*tensors, late=()):
        size = tensors[0].shape[0] // n_fsdp

        def block(m):
            parts = [tensor[m * size : (m + 1) * size] for tensor in tensors]
            return jnp.concatenate(parts, 1) if len(parts) > 1 else parts[0]

        total = block(0).astype(f32)
        for m in range(1, n_fsdp):
            total = total + after(across(block(m), m), *late).astype(f32)
        return total.astype(bf16)

    def gather_tokens(own):
        return lax.all_gather(own, ("ctx", "tp"), axis=0, tiled=True)

    def scatter_tokens(partial):
        return lax.psum_scatter(partial.astype(bf16), ("ctx", "tp"), scatter_dimension=0, tiled=True)

    order_row = span_order[0]
    positions = (
        order_row[:, None] * span_len + jnp.arange(span_len, dtype=jnp.int32)[None, :]
    ).reshape(-1)
    cosine, sine = rope_tables(positions)
    length = positions.shape[0]

    def own_rows(tensor):
        return reorder(lax.dynamic_slice_in_dim(tensor[0], t_at * span_len, span_len, 0))

    inputs_own = own_rows(block_in)
    cot_own = own_rows(cotangent)

    gains = jnp.stack([attn_gain, mlp_gain])
    gains = gather_plane_small(swap_small(gains, along, c_at, n_ctx), across, n_bits)
    gains_wide = gains.astype(f32)
    gain_one, gain_two = gains_wide[0], gains_wide[1]

    heads_width = w_query.shape[1] // n_ctx
    attn_part = after(swap_columns(w_query, w_key, w_value, w_out.T), gains)
    attn_pieces = plane_pieces(attn_part)
    attn_full = jnp.concatenate(attn_pieces, 0)
    gate_part = swap_columns(after(w_gate, attn_part))
    inputs_low = after(gather_tokens(after(inputs_own, attn_part)), gate_part, attn_full)
    qkv_full = attn_full[:, : 3 * heads_width]
    out_full = attn_full[:, 3 * heads_width :]

    heads_here = heads_width // HEAD_DIM
    normed_one, qkv = project(
        inputs_low, gain_one[None], cosine, sine, attn_pieces, heads_width, row_count
    )
    up_part = swap_columns(after(w_up, inputs_low), late=(qkv,))
    attn_low, log_total, peaks = attend(order_row, qkv)
    down_part = swap_columns(after(w_down.T, up_part))
    gate_full = gather_plane(after(gate_part, attn_full, inputs_low), late=(attn_low,))
    up_full = gather_plane(after(up_part, gate_full))
    down_full = gather_plane(after(down_part, up_full))
    attn_low = after(attn_low, up_part, gate_full)
    head_max = peaks[:, 0, ::HEAD_DIM].reshape(-1)
    attn_sum = scatter_tokens(dot_rt(attn_low, out_full))
    attn_sum = after(attn_sum, down_part, up_full)

    inputs_mine = inputs_own.astype(f32)
    resid = inputs_mine + attn_sum.astype(f32)
    inv_two = lax.rsqrt(jnp.mean(resid * resid, -1, keepdims=True) + NORM_EPS)
    scaled_two = resid * inv_two
    normed_mine = (scaled_two * gain_two).astype(bf16)
    normed_two = gather_tokens(normed_mine)
    cot_all = gather_tokens(after(cot_own, normed_mine))
    normed_two = after(normed_two, down_full)
    gate_act = dot(normed_two, gate_full)
    up_act = dot(normed_two, up_full)
    sig_gate = jax.nn.sigmoid(gate_act)
    silu_gate = gate_act * sig_gate
    hidden = (silu_gate * up_act).astype(bf16)
    mlp_partial = dot_rt(hidden, down_full).astype(bf16)
    mlp_sum = scatter_tokens(mlp_partial)
    grad_hidden = dot(after(cot_all, mlp_partial), down_full)
    silu_slope = sig_gate * (1.0 + gate_act * (1.0 - sig_gate))
    grad_gate = (grad_hidden * up_act * silu_slope).astype(bf16)
    grad_up = (grad_hidden * silu_gate).astype(bf16)
    back_two = (dot_rt(grad_gate, gate_full) + dot_rt(grad_up, up_full)).astype(bf16)
    hidden_late, gate_late, up_late = (after(g, back_two) for g in (hidden, grad_gate, grad_up))
    grad_w_down = dot_lt(cot_all, hidden_late).astype(bf16)
    back_two, mlp_sum = lax.optimization_barrier((back_two, mlp_sum))
    grad_normed_two = scatter_tokens(back_two)
    grad_w_gate = dot_lt(normed_two, gate_late).astype(bf16)
    grad_w_up = dot_lt(normed_two, up_late).astype(bf16)
    down_sum = scatter_plane(grad_w_down)
    grad_normed_two = after(grad_normed_two, down_sum, grad_w_gate, grad_w_up).astype(f32)

    grad_gain_two = jnp.sum(grad_normed_two * scaled_two, axis=0)
    weighted_two = grad_normed_two * gain_two
    grad_resid = cot_own.astype(f32) + inv_two * (
        weighted_two - scaled_two * jnp.mean(weighted_two * scaled_two, -1, keepdims=True)
    )
    grad_low = gather_tokens(grad_resid.astype(bf16))
    gate_sum = scatter_plane(after(grad_w_gate, down_sum))
    (down_out,) = swap_rows(down_sum, ("turned",))
    grad_low = after(grad_low, gate_sum, down_out)
    block_out_mine = (resid + mlp_sum.astype(f32)).astype(bf16)

    grad_attended = dot(grad_low, out_full).astype(bf16)
    grad_proj = attend_back(order_row, qkv, grad_attended, log_total, cosine, sine)
    up_sum = scatter_plane(after(grad_w_up, gate_sum), late=(grad_proj,))
    (gate_out,) = swap_rows(after(gate_sum, grad_low), ("side",), late=(grad_proj,))
    back_one = dot_rt(after(grad_proj, up_sum, gate_out), qkv_full).astype(bf16)
    grad_normed_one = scatter_tokens(back_one)
    proj_late, attn_late, back_late = (after(g, back_one) for g in (grad_proj, attn_low, back_one))
    grad_w_qkv = dot_lt(normed_one, proj_late).astype(bf16)
    grad_w_out = dot_lt(grad_low, attn_late).astype(bf16)
    (up_out,) = swap_rows(after(up_sum, back_one), ("side",))
    attn_weight_sum = scatter_plane(grad_w_qkv, grad_w_out, late=(up_out,))
    query_out, key_out, value_out, out_proj_out = swap_rows(
        attn_weight_sum, ("side", "side", "side", "turned")
    )
    inputs = inputs_low.astype(f32)
    inv_one = lax.rsqrt(jnp.mean(inputs * inputs, -1, keepdims=True) + NORM_EPS)
    back_late = after(back_late, grad_w_qkv, grad_w_out)
    grad_gain_one = jnp.sum(back_late.astype(f32) * (inputs * inv_one), axis=0)
    grad_normed_one = after(grad_normed_one, grad_w_qkv, grad_w_out).astype(f32)

    inv_mine = lax.rsqrt(jnp.mean(inputs_mine * inputs_mine, -1, keepdims=True) + NORM_EPS)
    scaled_one = inputs_mine * inv_mine
    weighted_one = grad_normed_one * gain_one
    input_grad_mine = grad_resid + inv_mine * (
        weighted_one - scaled_one * jnp.mean(weighted_one * scaled_one, -1, keepdims=True)
    )

    gain_grads = after(jnp.stack([grad_gain_one, grad_gain_two]), attn_weight_sum)
    gain_grads = gain_grads + twin(gain_grads)
    peak = head_max[None]
    held = {m: gain_grads[:, m * feature_block : (m + 1) * feature_block] for m in range(n_fsdp)}
    for bit in [1 << step for step in range(n_bits)]:
        kept = [m for m in sorted(held) if not m & bit]
        sent = [held[m | bit].reshape(1, -1) for m in kept]
        came = across(jnp.concatenate(sent + [peak], 1), bit)
        size = 2 * feature_block
        held = {
            m: held[m] + came[:, at * size : (at + 1) * size].reshape(2, feature_block)
            for at, m in enumerate(kept)
        }
        peak = jnp.maximum(peak, came[:, len(kept) * size :])
    piece = feature_block // n_ctx
    gain_total = None
    head_peak = jnp.zeros((n_ctx * heads_here,), f32)
    for shift in range(n_ctx):
        sent = lax.dynamic_slice_in_dim(held[0], ((c_at + shift) % n_ctx) * piece, piece, 1)
        came = along(jnp.concatenate([sent.reshape(1, -1), peak], 1), shift)
        part = came[:, : 2 * piece].reshape(2, piece)
        gain_total = part if gain_total is None else gain_total + part
        head_peak = lax.dynamic_update_slice_in_dim(
            head_peak, came[0, 2 * piece :], ((c_at - shift) % n_ctx) * heads_here, 0
        )

    def both_cores(mine):
        mine = reorder(mine)
        other = twin(mine)
        first = jnp.where(t_at == 0, mine, other)
        second = jnp.where(t_at == 0, other, mine)
        return jnp.concatenate([first, second], 0)[None]

    factor = jnp.sqrt(clip_limit / jnp.maximum(clip_limit, head_peak))
    column_factor = jnp.repeat(factor, HEAD_DIM)
    clipped_query = w_query.astype(f32) * column_factor[None, :]
    clipped_key = w_key.astype(f32) * column_factor[None, :]
    return (
        both_cores(block_out_mine),
        both_cores(input_grad_mine),
        gain_total[0],
        query_out,
        key_out,
        value_out,
        out_proj_out,
        gain_total[1],
        gate_out,
        up_out,
        down_out,
        head_peak,
        clipped_query,
        clipped_key,
    )


def swap_small(gains, along, c_at, n_ctx):
    piece = gains.shape[1]
    placed = jnp.zeros((gains.shape[0], piece * n_ctx), gains.dtype)
    for shift in range(n_ctx):
        placed = lax.dynamic_update_slice_in_dim(
            placed, along(gains, shift), ((c_at - shift) % n_ctx) * piece, 1
        )
    return placed


def gather_plane_small(gains, across, n_bits):
    for step in range(n_bits):
        gains = jnp.concatenate([gains, across(gains, 1 << step)], 1)
    return gains


def solution(mesh):
    placed = (
        P("fsdp", "ctx", None),
        P("fsdp", None),
        P(("fsdp", "ctx")),
        P(("fsdp", "ctx"), "tp"),
        P(("fsdp", "ctx"), "tp"),
        P(("fsdp", "ctx"), "tp"),
        P("tp", ("fsdp", "ctx")),
        P(("fsdp", "ctx")),
        P(("fsdp", "ctx"), "tp"),
        P(("fsdp", "ctx"), "tp"),
        P("tp", ("fsdp", "ctx")),
        P("tp"),
        P("fsdp", "ctx", None),
    )
    return jax.shard_map(
        on_device,
        mesh=mesh,
        in_specs=placed,
        out_specs=(
            P("fsdp", "ctx", None),
            P("fsdp", "ctx", None),
            P(("fsdp", "ctx")),
            P(("fsdp", "ctx"), "tp"),
            P(("fsdp", "ctx"), "tp"),
            P(("fsdp", "ctx"), "tp"),
            P("tp", ("fsdp", "ctx")),
            P(("fsdp", "ctx")),
            P(("fsdp", "ctx"), "tp"),
            P(("fsdp", "ctx"), "tp"),
            P("tp", ("fsdp", "ctx")),
            P("tp"),
            P(("fsdp", "ctx"), "tp"),
            P(("fsdp", "ctx"), "tp"),
        ),
        check_vma=False,
    )
```

```python
import functools

import jax
import jax.numpy as jnp
from jax import lax
from jax.experimental import pallas as pl
from jax.experimental.pallas import tpu as pltpu
from jax.sharding import PartitionSpec as P

HEAD_DIM = 64
NORM_EPS = 1e-05
ROPE_BASE = 130000.0

f32 = jnp.float32
bf16 = jnp.bfloat16

PAIR = 2 * HEAD_DIM
ROWS = 256
VMEM_LIMIT = 48 * 1024 * 1024


def rope_tables(positions):
    half_dim = HEAD_DIM // 2
    step_index = jnp.arange(half_dim, dtype=f32)
    frequency = jnp.power(ROPE_BASE, -2.0 * step_index / (2 * half_dim))
    angles = positions.astype(f32)[:, None] * frequency[None, :]
    cosine, sine = jnp.cos(angles), jnp.sin(angles)
    return (
        jnp.concatenate([cosine, cosine, cosine, cosine], 1),
        jnp.concatenate([-sine, sine, -sine, sine], 1),
    )


def dot(left, right):
    return jnp.dot(left, right, preferred_element_type=f32)


def dot_lt(left, right):
    return lax.dot_general(left, right, (((0,), (0,)), ((), ())), preferred_element_type=f32)


def dot_rt(left, right):
    return lax.dot_general(left, right, (((1,), (1,)), ((), ())), preferred_element_type=f32)


def place_kernel(count, ways, at_ref, *refs):
    pieces = len(refs) - count
    slot = lax.rem(at_ref[0] + pieces - pl.program_id(0), pieces)
    for at in range(pieces):

        @pl.when(slot == at)
        def _(source=refs[at]):
            columns = source.shape[1] // count
            for which in range(count):
                part = source[:, which * columns : (which + 1) * columns]
                target = refs[pieces + which]
                part = part.astype(target.dtype)
                target[...] = part.T if ways[which] == "turned" else part


def place(at, pieces, count, ways, dtype):
    slots = len(pieces)
    rows, columns = pieces[0].shape
    columns = columns // count
    shapes = {
        "down": ((slots * rows, columns), (rows, columns), lambda b, at: (b, 0)),
        "side": ((rows, slots * columns), (rows, columns), lambda b, at: (0, b)),
        "turned": ((slots * columns, rows), (columns, rows), lambda b, at: (b, 0)),
    }
    return pl.pallas_call(
        functools.partial(place_kernel, count, ways),
        grid_spec=pltpu.PrefetchScalarGridSpec(
            num_scalar_prefetch=1,
            grid=(slots,),
            in_specs=[pl.BlockSpec(piece.shape, lambda b, at: (0, 0)) for piece in pieces],
            out_specs=[pl.BlockSpec(shapes[way][1], shapes[way][2]) for way in ways],
        ),
        out_shape=[jax.ShapeDtypeStruct(shapes[way][0], dtype) for way in ways],
        compiler_params=pltpu.CompilerParams(vmem_limit_bytes=VMEM_LIMIT),
        cost_estimate=pl.CostEstimate(
            flops=0, bytes_accessed=6 * slots * rows * columns * count, transcendentals=0
        ),
        name="place",
    )(at.astype(jnp.int32)[None], *pieces)


def turn(pair, cosine, sine):
    lane = lax.broadcasted_iota(jnp.int32, pair.shape, 1)
    half_dim = HEAD_DIM // 2
    swapped = jnp.where(
        lane % HEAD_DIM < half_dim,
        pltpu.roll(pair, PAIR - half_dim, 1),
        pltpu.roll(pair, half_dim, 1),
    )
    return pair * cosine + swapped * sine


def project_kernel(pieces, heads_width, x_ref, gain_ref, cosine_ref, sine_ref, *refs):
    weights, normed_ref, out_ref = refs[:pieces], refs[pieces], refs[pieces + 1]
    inputs = x_ref[...].astype(f32)
    inverse = lax.rsqrt(jnp.mean(inputs * inputs, -1, keepdims=True) + NORM_EPS)
    normed = (inputs * inverse * gain_ref[...]).astype(bf16)
    normed_ref[...] = normed
    block = normed.shape[1] // pieces
    proj = None
    for at, weight in enumerate(weights):
        term = dot(normed[:, at * block : (at + 1) * block], weight[:, : 3 * heads_width])
        proj = term if proj is None else proj + term
    cosine, sine = cosine_ref[...], sine_ref[...]
    for at in range(3 * heads_width // PAIR):
        pair = proj[:, at * PAIR : (at + 1) * PAIR]
        if at < 2 * heads_width // PAIR:
            pair = turn(pair, cosine, sine)
        out_ref[:, at * PAIR : (at + 1) * PAIR] = pair.astype(bf16)


def project(tokens, gain, cosine, sine, weights, heads_width, row_block):
    length, width = tokens.shape
    rows = lambda columns: pl.BlockSpec((row_block, columns), lambda i: (i, 0))
    whole = lambda tensor: pl.BlockSpec(tensor.shape, lambda i: (0, 0))
    return pl.pallas_call(
        functools.partial(project_kernel, len(weights), heads_width),
        grid=(length // row_block,),
        out_shape=(
            jax.ShapeDtypeStruct((length, width), bf16),
            jax.ShapeDtypeStruct((length, 3 * heads_width), bf16),
        ),
        in_specs=[rows(width), whole(gain), rows(PAIR), rows(PAIR)] + [whole(w) for w in weights],
        out_specs=(rows(width), rows(3 * heads_width)),
        compiler_params=pltpu.CompilerParams(vmem_limit_bytes=VMEM_LIMIT),
        cost_estimate=pl.CostEstimate(
            flops=length * width * heads_width,
            bytes_accessed=4 * length * width + 8 * width * heads_width,
            transcendentals=length,
        ),
        name="project",
    )(tokens, gain, cosine, sine, *weights)


def sort_spans(order_ref, source, sorted_ref):
    span = sorted_ref.shape[0] // order_ref.shape[0]
    for at in range(order_ref.shape[0]):
        start = pl.multiple_of(order_ref[at] * span, span)
        sorted_ref[pl.ds(start, span), :] = source[at * span : (at + 1) * span, :]


def unsorted_span(order_ref, sorted_ref, at):
    span = sorted_ref.shape[0] // order_ref.shape[0]
    start = pl.multiple_of(order_ref[at] * span, span)
    return sorted_ref[pl.ds(start, span), :]


def causal(scores, first_row):
    row = lax.broadcasted_iota(jnp.int32, scores.shape, 0) + first_row
    column = lax.broadcasted_iota(jnp.int32, scores.shape, 1)
    return jnp.where(column <= row, scores, -1e30)


def forward_kernel(order_ref, q_ref, k_ref, v_ref, out_ref, log_ref, peak_ref, q_s, k_s, v_s, o_s):
    length = q_ref.shape[0]
    block = min(ROWS, length)
    scale = HEAD_DIM ** (-0.5)
    for source, held in ((q_ref, q_s), (k_ref, k_s), (v_ref, v_s)):
        sort_spans(order_ref, source, held)
    lane = lax.broadcasted_iota(jnp.int32, (block, PAIR), 1)
    peaks = [None, None]
    for start in range(0, length, block):
        end = start + block
        query, key, value = q_s[start:end, :], k_s[:end, :], v_s[:end, :]
        attended, logs = [], []
        for head in range(2):
            mine = (lane // HEAD_DIM) == head
            scores = causal(dot_rt(jnp.where(mine, query, 0), key) * scale, start)
            row_max = jnp.max(scores, 1, keepdims=True)
            terms = jnp.exp(scores - row_max)
            total = jnp.sum(terms, 1, keepdims=True)
            attended.append(dot((terms * (1.0 / total)).astype(bf16), value))
            logs.append(row_max + jnp.log(total))
            top = jnp.max(row_max)
            peaks[head] = top if peaks[head] is None else jnp.maximum(peaks[head], top)
        o_s[start:end, :] = jnp.where(lane < HEAD_DIM, attended[0], attended[1])
        log_ref[0, start:end, :] = jnp.where(lane < HEAD_DIM, logs[0], logs[1])
    for at in range(order_ref.shape[0]):
        span = length // order_ref.shape[0]
        out_ref[at * span : (at + 1) * span, :] = unsorted_span(order_ref, o_s, at).astype(bf16)
    lane = lax.broadcasted_iota(jnp.int32, peak_ref.shape, 2)
    peak_ref[...] = jnp.where(lane < HEAD_DIM, peaks[0], peaks[1])


def attend(order, qkv):
    length = qkv.shape[0]
    pairs = qkv.shape[1] // (3 * PAIR)
    column = lambda first: pl.BlockSpec((length, PAIR), lambda g, order: (0, first + g))
    return pl.pallas_call(
        forward_kernel,
        grid_spec=pltpu.PrefetchScalarGridSpec(
            num_scalar_prefetch=1,
            grid=(pairs,),
            in_specs=[column(0), column(pairs), column(2 * pairs)],
            out_specs=(
                column(0),
                pl.BlockSpec((1, length, PAIR), lambda g, order: (g, 0, 0)),
                pl.BlockSpec((1, 8, PAIR), lambda g, order: (g, 0, 0)),
            ),
            scratch_shapes=[pltpu.VMEM((length, PAIR), bf16)] * 3 + [pltpu.VMEM((length, PAIR), f32)],
        ),
        out_shape=(
            jax.ShapeDtypeStruct((length, pairs * PAIR), bf16),
            jax.ShapeDtypeStruct((pairs, length, PAIR), f32),
            jax.ShapeDtypeStruct((pairs, 8, PAIR), f32),
        ),
        compiler_params=pltpu.CompilerParams(vmem_limit_bytes=VMEM_LIMIT),
        cost_estimate=pl.CostEstimate(
            flops=2 * pairs * length * length * PAIR,
            bytes_accessed=8 * pairs * length * PAIR,
            transcendentals=pairs * length,
        ),
        name="attend",
    )(order, qkv, qkv, qkv)


def backward_kernel(
    order_ref, q_ref, k_ref, v_ref, g_ref, log_ref, cosine_ref, sine_ref, out_ref, *held
):
    q_s, k_s, v_s, g_s, dq_s, dk_s, dv_s = held
    length = q_ref.shape[0]
    block = min(ROWS, length)
    scale = HEAD_DIM ** (-0.5)
    for source, into in ((q_ref, q_s), (k_ref, k_s), (v_ref, v_s), (g_ref, g_s)):
        sort_spans(order_ref, source, into)
    dk_s[...] = jnp.zeros_like(dk_s)
    dv_s[...] = jnp.zeros_like(dv_s)
    lane = lax.broadcasted_iota(jnp.int32, (block, PAIR), 1)
    for start in range(0, length, block):
        end = start + block
        query, grad = q_s[start:end, :], g_s[start:end, :]
        key, value = k_s[:end, :], v_s[:end, :]
        grad_query = []
        for head in range(2):
            mine = (lane // HEAD_DIM) == head
            query_h = jnp.where(mine, query, 0)
            grad_h = jnp.where(mine, grad, 0)
            log_h = log_ref[0, start:end, head * HEAD_DIM : head * HEAD_DIM + 1]
            scores = causal(dot_rt(query_h, key) * scale, start)
            prob = jnp.exp(scores - log_h)
            grad_prob = dot_rt(grad_h, value)
            delta = jnp.sum(prob * grad_prob, 1, keepdims=True)
            grad_score = (prob * (grad_prob - delta)).astype(bf16)
            grad_query.append(dot(grad_score, key))
            dk_s[:end, :] += dot_lt(grad_score, query_h)
            dv_s[:end, :] += dot_lt(prob.astype(bf16), grad_h)
        dq_s[start:end, :] = jnp.where(lane < HEAD_DIM, grad_query[0], grad_query[1])
    pairs = out_ref.shape[1] // (3 * PAIR)
    column = pl.program_id(0)
    span = length // order_ref.shape[0]
    for at in range(order_ref.shape[0]):
        rows = slice(at * span, (at + 1) * span)
        cosine, sine = cosine_ref[rows, :], sine_ref[rows, :]
        for which, source in enumerate((dq_s, dk_s, dv_s)):
            part = unsorted_span(order_ref, source, at)
            if which < 2:
                part = turn(part * scale, cosine, -sine)
            start = pl.multiple_of((which * pairs + column) * PAIR, PAIR)
            out_ref[rows, pl.ds(start, PAIR)] = part.astype(bf16)


def attend_back(order, qkv, grad, logs, cosine, sine):
    length = qkv.shape[0]
    pairs = qkv.shape[1] // (3 * PAIR)
    column = lambda first: pl.BlockSpec((length, PAIR), lambda g, order: (0, first + g))
    whole = pl.BlockSpec((length, PAIR), lambda g, order: (0, 0))
    return pl.pallas_call(
        backward_kernel,
        grid_spec=pltpu.PrefetchScalarGridSpec(
            num_scalar_prefetch=1,
            grid=(pairs,),
            in_specs=[
                column(0),
                column(pairs),
                column(2 * pairs),
                column(0),
                pl.BlockSpec((1, length, PAIR), lambda g, order: (g, 0, 0)),
                whole,
                whole,
            ],
            out_specs=pl.BlockSpec((length, 3 * pairs * PAIR), lambda g, order: (0, 0)),
            scratch_shapes=[pltpu.VMEM((length, PAIR), bf16)] * 4
            + [pltpu.VMEM((length, PAIR), f32)] * 3,
        ),
        out_shape=jax.ShapeDtypeStruct(qkv.shape, bf16),
        compiler_params=pltpu.CompilerParams(vmem_limit_bytes=VMEM_LIMIT),
        cost_estimate=pl.CostEstimate(
            flops=2 * pairs * length * length * PAIR,
            bytes_accessed=16 * pairs * length * PAIR,
            transcendentals=pairs * length,
        ),
        name="attend_back",
    )(order, qkv, qkv, qkv, grad, logs, cosine, sine)


def on_device(
    block_in,
    span_order,
    attn_gain,
    w_query,
    w_key,
    w_value,
    w_out,
    mlp_gain,
    w_gate,
    w_up,
    w_down,
    clip_limit,
    cotangent,
):
    n_ctx = lax.axis_size("ctx")
    n_fsdp = lax.axis_size("fsdp")
    n_bits = n_fsdp.bit_length() - 1
    c_at = lax.axis_index("ctx")
    f_at = lax.axis_index("fsdp")
    t_at = lax.axis_index("tp")
    row_count, width = block_in.shape[1:]
    span_len = row_count // 2
    feature_block = width // n_fsdp

    def along(tensor, shift):
        if shift % n_ctx == 0:
            return tensor
        return lax.ppermute(tensor, "ctx", [(i, (i + shift) % n_ctx) for i in range(n_ctx)])

    def across(tensor, mask):
        return lax.ppermute(tensor, "fsdp", [(i, i ^ mask) for i in range(n_fsdp)])

    def twin(tensor):
        return lax.ppermute(tensor, "tp", [(0, 1), (1, 0)])

    def after(tensor, *earlier):
        return lax.optimization_barrier((tensor, *earlier))[0]

    def reorder(tensor):
        return jnp.concatenate(
            [
                lax.dynamic_slice_in_dim(tensor, (f_at ^ m) * feature_block, feature_block, -1)
                for m in range(n_fsdp)
            ],
            -1,
        )

    def swap_columns(*tensors, late=()):
        piece = tensors[0].shape[1] // n_ctx
        came = []
        for shift in range(n_ctx):
            start = ((c_at + shift) % n_ctx) * piece
            sent = [lax.dynamic_slice_in_dim(tensor, start, piece, 1) for tensor in tensors]
            came.append(after(along(jnp.concatenate(sent, 1), shift), *late))
        return place(c_at, came, 1, ("down",), bf16)[0]

    def swap_rows(tensor, ways, late=()):
        piece = tensor.shape[0] // n_ctx
        came = []
        for shift in range(n_ctx):
            sent = lax.dynamic_slice_in_dim(tensor, ((c_at + shift) % n_ctx) * piece, piece, 0)
            came.append(after(along(sent, shift), *late))
        return place(c_at, came, len(ways), ways, f32)

    def plane_pieces(tensor, late=()):
        if n_fsdp != 4:
            return [tensor] + [after(across(tensor, m), *late) for m in range(1, n_fsdp)]
        half = tensor.shape[0] // 2
        near_x, near_y = across(tensor, 1), across(tensor, 2)
        far = [across(near_x[:half], 2), across(near_y[half:], 1)]
        pieces = [tensor, near_x, near_y, jnp.concatenate(far, 0)]
        return [after(piece, *late) for piece in pieces]

    def gather_plane(tensor, late=()):
        return jnp.concatenate(plane_pieces(tensor, late), 0)

    def scatter_plane(*tensors, late=()):
        size = tensors[0].shape[0] // n_fsdp

        def block(m):
            parts = [tensor[m * size : (m + 1) * size] for tensor in tensors]
            return jnp.concatenate(parts, 1) if len(parts) > 1 else parts[0]

        total = block(0).astype(f32)
        for m in range(1, n_fsdp):
            total = total + after(across(block(m), m), *late).astype(f32)
        return total.astype(bf16)

    def gather_tokens(own):
        return lax.all_gather(own, ("ctx", "tp"), axis=0, tiled=True)

    def scatter_tokens(partial):
        return lax.psum_scatter(partial.astype(bf16), ("ctx", "tp"), scatter_dimension=0, tiled=True)

    order_row = span_order[0]
    positions = (
        order_row[:, None] * span_len + jnp.arange(span_len, dtype=jnp.int32)[None, :]
    ).reshape(-1)
    cosine, sine = rope_tables(positions)
    length = positions.shape[0]

    def own_rows(tensor):
        return reorder(lax.dynamic_slice_in_dim(tensor[0], t_at * span_len, span_len, 0))

    inputs_own = own_rows(block_in)
    cot_own = own_rows(cotangent)

    gains = jnp.stack([attn_gain, mlp_gain])
    gains = gather_plane_small(swap_small(gains, along, c_at, n_ctx), across, n_bits)
    gains_wide = gains.astype(f32)
    gain_one, gain_two = gains_wide[0], gains_wide[1]

    heads_width = w_query.shape[1] // n_ctx
    attn_part = after(swap_columns(w_query, w_key, w_value, w_out.T), gains)
    attn_pieces = plane_pieces(attn_part)
    attn_full = jnp.concatenate(attn_pieces, 0)
    inputs_low = after(gather_tokens(after(inputs_own, attn_part)), attn_full)
    qkv_full = attn_full[:, : 3 * heads_width]
    out_full = attn_full[:, 3 * heads_width :]

    heads_here = heads_width // HEAD_DIM
    normed_one, qkv = project(
        inputs_low, gain_one[None], cosine, sine, attn_pieces, heads_width, row_count
    )
    gate_part = swap_columns(after(w_gate, inputs_low), late=(qkv,))
    up_part = swap_columns(after(w_up, inputs_low), late=(qkv,))
    qkv = after(qkv, gate_part)
    attn_low, log_total, peaks = attend(order_row, qkv)
    down_part = swap_columns(after(w_down.T, up_part))
    gate_full = gather_plane(gate_part, late=(attn_low,))
    up_full = gather_plane(after(up_part, gate_full))
    down_full = gather_plane(after(down_part, up_full))
    attn_low = after(attn_low, up_part, gate_full)
    head_max = peaks[:, 0, ::HEAD_DIM].reshape(-1)
    attn_sum = scatter_tokens(dot_rt(attn_low, out_full))
    attn_sum = after(attn_sum, down_part, up_full)

    inputs_mine = inputs_own.astype(f32)
    resid = inputs_mine + attn_sum.astype(f32)
    inv_two = lax.rsqrt(jnp.mean(resid * resid, -1, keepdims=True) + NORM_EPS)
    scaled_two = resid * inv_two
    normed_mine = (scaled_two * gain_two).astype(bf16)
    normed_two = gather_tokens(normed_mine)
    cot_all = gather_tokens(after(cot_own, normed_mine))
    normed_two = after(normed_two, down_full)
    gate_act = dot(normed_two, gate_full)
    up_act = dot(normed_two, up_full)
    sig_gate = jax.nn.sigmoid(gate_act)
    silu_gate = gate_act * sig_gate
    hidden = (silu_gate * up_act).astype(bf16)
    mlp_partial = dot_rt(hidden, down_full).astype(bf16)
    mlp_sum = scatter_tokens(mlp_partial)
    grad_hidden = dot(after(cot_all, mlp_partial), down_full)
    silu_slope = sig_gate * (1.0 + gate_act * (1.0 - sig_gate))
    grad_gate = (grad_hidden * up_act * silu_slope).astype(bf16)
    grad_up = (grad_hidden * silu_gate).astype(bf16)
    back_two = (dot_rt(grad_gate, gate_full) + dot_rt(grad_up, up_full)).astype(bf16)
    hidden_late, gate_late, up_late = (after(g, back_two) for g in (hidden, grad_gate, grad_up))
    grad_w_down = dot_lt(cot_all, hidden_late).astype(bf16)
    back_two, mlp_sum = lax.optimization_barrier((back_two, mlp_sum))
    grad_normed_two = scatter_tokens(back_two)
    grad_w_gate = dot_lt(normed_two, gate_late).astype(bf16)
    grad_w_up = dot_lt(normed_two, up_late).astype(bf16)
    down_sum = scatter_plane(grad_w_down)
    grad_normed_two = after(grad_normed_two, down_sum, grad_w_gate, grad_w_up).astype(f32)

    grad_gain_two = jnp.sum(grad_normed_two * scaled_two, axis=0)
    weighted_two = grad_normed_two * gain_two
    grad_resid = cot_own.astype(f32) + inv_two * (
        weighted_two - scaled_two * jnp.mean(weighted_two * scaled_two, -1, keepdims=True)
    )
    grad_low = gather_tokens(grad_resid.astype(bf16))
    gate_sum = scatter_plane(after(grad_w_gate, down_sum))
    (down_out,) = swap_rows(down_sum, ("turned",))
    grad_low = after(grad_low, gate_sum, down_out)
    block_out_mine = (resid + mlp_sum.astype(f32)).astype(bf16)

    grad_attended = dot(grad_low, out_full).astype(bf16)
    grad_proj = attend_back(order_row, qkv, grad_attended, log_total, cosine, sine)
    up_sum = scatter_plane(after(grad_w_up, gate_sum), late=(grad_proj,))
    (gate_out,) = swap_rows(after(gate_sum, grad_low), ("side",), late=(grad_proj,))
    back_one = dot_rt(after(grad_proj, up_sum, gate_out), qkv_full).astype(bf16)
    grad_normed_one = scatter_tokens(back_one)
    proj_late, attn_late, back_late = (after(g, back_one) for g in (grad_proj, attn_low, back_one))
    grad_w_qkv = dot_lt(normed_one, proj_late).astype(bf16)
    grad_w_out = dot_lt(grad_low, attn_late).astype(bf16)
    (up_out,) = swap_rows(after(up_sum, back_one), ("side",))
    attn_weight_sum = scatter_plane(grad_w_qkv, grad_w_out, late=(up_out,))
    query_out, key_out, value_out, out_proj_out = swap_rows(
        attn_weight_sum, ("side", "side", "side", "turned")
    )
    inputs = inputs_low.astype(f32)
    inv_one = lax.rsqrt(jnp.mean(inputs * inputs, -1, keepdims=True) + NORM_EPS)
    back_late = after(back_late, grad_w_qkv, grad_w_out)
    grad_gain_one = jnp.sum(back_late.astype(f32) * (inputs * inv_one), axis=0)
    grad_normed_one = after(grad_normed_one, grad_w_qkv, grad_w_out).astype(f32)

    inv_mine = lax.rsqrt(jnp.mean(inputs_mine * inputs_mine, -1, keepdims=True) + NORM_EPS)
    scaled_one = inputs_mine * inv_mine
    weighted_one = grad_normed_one * gain_one
    input_grad_mine = grad_resid + inv_mine * (
        weighted_one - scaled_one * jnp.mean(weighted_one * scaled_one, -1, keepdims=True)
    )

    gain_grads = after(jnp.stack([grad_gain_one, grad_gain_two]), attn_weight_sum)
    gain_grads = gain_grads + twin(gain_grads)
    peak = head_max[None]
    held = {m: gain_grads[:, m * feature_block : (m + 1) * feature_block] for m in range(n_fsdp)}
    for bit in [1 << step for step in range(n_bits)]:
        kept = [m for m in sorted(held) if not m & bit]
        sent = [held[m | bit].reshape(1, -1) for m in kept]
        came = across(jnp.concatenate(sent + [peak], 1), bit)
        size = 2 * feature_block
        held = {
            m: held[m] + came[:, at * size : (at + 1) * size].reshape(2, feature_block)
            for at, m in enumerate(kept)
        }
        peak = jnp.maximum(peak, came[:, len(kept) * size :])
    piece = feature_block // n_ctx
    gain_total = None
    head_peak = jnp.zeros((n_ctx * heads_here,), f32)
    for shift in range(n_ctx):
        sent = lax.dynamic_slice_in_dim(held[0], ((c_at + shift) % n_ctx) * piece, piece, 1)
        came = along(jnp.concatenate([sent.reshape(1, -1), peak], 1), shift)
        part = came[:, : 2 * piece].reshape(2, piece)
        gain_total = part if gain_total is None else gain_total + part
        head_peak = lax.dynamic_update_slice_in_dim(
            head_peak, came[0, 2 * piece :], ((c_at - shift) % n_ctx) * heads_here, 0
        )

    def both_cores(mine):
        mine = reorder(mine)
        other = twin(mine)
        first = jnp.where(t_at == 0, mine, other)
        second = jnp.where(t_at == 0, other, mine)
        return jnp.concatenate([first, second], 0)[None]

    factor = jnp.sqrt(clip_limit / jnp.maximum(clip_limit, head_peak))
    column_factor = jnp.repeat(factor, HEAD_DIM)
    clipped_query = w_query.astype(f32) * column_factor[None, :]
    clipped_key = w_key.astype(f32) * column_factor[None, :]
    return (
        both_cores(block_out_mine),
        both_cores(input_grad_mine),
        gain_total[0],
        query_out,
        key_out,
        value_out,
        out_proj_out,
        gain_total[1],
        gate_out,
        up_out,
        down_out,
        head_peak,
        clipped_query,
        clipped_key,
    )


def swap_small(gains, along, c_at, n_ctx):
    piece = gains.shape[1]
    placed = jnp.zeros((gains.shape[0], piece * n_ctx), gains.dtype)
    for shift in range(n_ctx):
        placed = lax.dynamic_update_slice_in_dim(
            placed, along(gains, shift), ((c_at - shift) % n_ctx) * piece, 1
        )
    return placed


def gather_plane_small(gains, across, n_bits):
    for step in range(n_bits):
        gains = jnp.concatenate([gains, across(gains, 1 << step)], 1)
    return gains


def solution(mesh):
    placed = (
        P("fsdp", "ctx", None),
        P("fsdp", None),
        P(("fsdp", "ctx")),
        P(("fsdp", "ctx"), "tp"),
        P(("fsdp", "ctx"), "tp"),
        P(("fsdp", "ctx"), "tp"),
        P("tp", ("fsdp", "ctx")),
        P(("fsdp", "ctx")),
        P(("fsdp", "ctx"), "tp"),
        P(("fsdp", "ctx"), "tp"),
        P("tp", ("fsdp", "ctx")),
        P("tp"),
        P("fsdp", "ctx", None),
    )
    return jax.shard_map(
        on_device,
        mesh=mesh,
        in_specs=placed,
        out_specs=(
            P("fsdp", "ctx", None),
            P("fsdp", "ctx", None),
            P(("fsdp", "ctx")),
            P(("fsdp", "ctx"), "tp"),
            P(("fsdp", "ctx"), "tp"),
            P(("fsdp", "ctx"), "tp"),
            P("tp", ("fsdp", "ctx")),
            P(("fsdp", "ctx")),
            P(("fsdp", "ctx"), "tp"),
            P(("fsdp", "ctx"), "tp"),
            P("tp", ("fsdp", "ctx")),
            P("tp"),
            P(("fsdp", "ctx"), "tp"),
            P(("fsdp", "ctx"), "tp"),
        ),
        check_vma=False,
    )
```

```python
import functools

import jax
import jax.numpy as jnp
from jax import lax
from jax.experimental import pallas as pl
from jax.experimental.pallas import tpu as pltpu
from jax.sharding import PartitionSpec as P

HEAD_DIM = 64
NORM_EPS = 1e-05
ROPE_BASE = 130000.0

f32 = jnp.float32
bf16 = jnp.bfloat16

PAIR = 2 * HEAD_DIM
ROWS = 256
VMEM_LIMIT = 48 * 1024 * 1024


def rope_tables(positions):
    half_dim = HEAD_DIM // 2
    step_index = jnp.arange(half_dim, dtype=f32)
    frequency = jnp.power(ROPE_BASE, -2.0 * step_index / (2 * half_dim))
    angles = positions.astype(f32)[:, None] * frequency[None, :]
    cosine, sine = jnp.cos(angles), jnp.sin(angles)
    return (
        jnp.concatenate([cosine, cosine, cosine, cosine], 1),
        jnp.concatenate([-sine, sine, -sine, sine], 1),
    )


def dot(left, right):
    return jnp.dot(left, right, preferred_element_type=f32)


def dot_lt(left, right):
    return lax.dot_general(left, right, (((0,), (0,)), ((), ())), preferred_element_type=f32)


def dot_rt(left, right):
    return lax.dot_general(left, right, (((1,), (1,)), ((), ())), preferred_element_type=f32)


def place_kernel(count, ways, at_ref, *refs):
    pieces = len(refs) - count
    slot = lax.rem(at_ref[0] + pieces - pl.program_id(0), pieces)
    for at in range(pieces):

        @pl.when(slot == at)
        def _(source=refs[at]):
            columns = source.shape[1] // count
            for which in range(count):
                part = source[:, which * columns : (which + 1) * columns]
                target = refs[pieces + which]
                part = part.astype(target.dtype)
                target[...] = part.T if ways[which] == "turned" else part


def place(at, pieces, count, ways, dtype):
    slots = len(pieces)
    rows, columns = pieces[0].shape
    columns = columns // count
    shapes = {
        "down": ((slots * rows, columns), (rows, columns), lambda b, at: (b, 0)),
        "side": ((rows, slots * columns), (rows, columns), lambda b, at: (0, b)),
        "turned": ((slots * columns, rows), (columns, rows), lambda b, at: (b, 0)),
    }
    return pl.pallas_call(
        functools.partial(place_kernel, count, ways),
        grid_spec=pltpu.PrefetchScalarGridSpec(
            num_scalar_prefetch=1,
            grid=(slots,),
            in_specs=[pl.BlockSpec(piece.shape, lambda b, at: (0, 0)) for piece in pieces],
            out_specs=[pl.BlockSpec(shapes[way][1], shapes[way][2]) for way in ways],
        ),
        out_shape=[jax.ShapeDtypeStruct(shapes[way][0], dtype) for way in ways],
        compiler_params=pltpu.CompilerParams(vmem_limit_bytes=VMEM_LIMIT),
        cost_estimate=pl.CostEstimate(
            flops=0, bytes_accessed=6 * slots * rows * columns * count, transcendentals=0
        ),
        name="place",
    )(at.astype(jnp.int32)[None], *pieces)


def turn(pair, cosine, sine):
    lane = lax.broadcasted_iota(jnp.int32, pair.shape, 1)
    half_dim = HEAD_DIM // 2
    swapped = jnp.where(
        lane % HEAD_DIM < half_dim,
        pltpu.roll(pair, PAIR - half_dim, 1),
        pltpu.roll(pair, half_dim, 1),
    )
    return pair * cosine + swapped * sine


def project_kernel(pieces, heads_width, x_ref, gain_ref, cosine_ref, sine_ref, *refs):
    weights, normed_ref, out_ref = refs[:pieces], refs[pieces], refs[pieces + 1]
    inputs = x_ref[...].astype(f32)
    inverse = lax.rsqrt(jnp.mean(inputs * inputs, -1, keepdims=True) + NORM_EPS)
    normed = (inputs * inverse * gain_ref[...]).astype(bf16)
    normed_ref[...] = normed
    block = normed.shape[1] // pieces
    proj = None
    for at, weight in enumerate(weights):
        term = dot(normed[:, at * block : (at + 1) * block], weight[:, : 3 * heads_width])
        proj = term if proj is None else proj + term
    cosine, sine = cosine_ref[...], sine_ref[...]
    for at in range(3 * heads_width // PAIR):
        pair = proj[:, at * PAIR : (at + 1) * PAIR]
        if at < 2 * heads_width // PAIR:
            pair = turn(pair, cosine, sine)
        out_ref[:, at * PAIR : (at + 1) * PAIR] = pair.astype(bf16)


def project(tokens, gain, cosine, sine, weights, heads_width, row_block):
    length, width = tokens.shape
    rows = lambda columns: pl.BlockSpec((row_block, columns), lambda i: (i, 0))
    whole = lambda tensor: pl.BlockSpec(tensor.shape, lambda i: (0, 0))
    return pl.pallas_call(
        functools.partial(project_kernel, len(weights), heads_width),
        grid=(length // row_block,),
        out_shape=(
            jax.ShapeDtypeStruct((length, width), bf16),
            jax.ShapeDtypeStruct((length, 3 * heads_width), bf16),
        ),
        in_specs=[rows(width), whole(gain), rows(PAIR), rows(PAIR)] + [whole(w) for w in weights],
        out_specs=(rows(width), rows(3 * heads_width)),
        compiler_params=pltpu.CompilerParams(vmem_limit_bytes=VMEM_LIMIT),
        cost_estimate=pl.CostEstimate(
            flops=length * width * heads_width,
            bytes_accessed=4 * length * width + 8 * width * heads_width,
            transcendentals=length,
        ),
        name="project",
    )(tokens, gain, cosine, sine, *weights)


def sort_spans(order_ref, source, sorted_ref):
    span = sorted_ref.shape[0] // order_ref.shape[0]
    for at in range(order_ref.shape[0]):
        start = pl.multiple_of(order_ref[at] * span, span)
        sorted_ref[pl.ds(start, span), :] = source[at * span : (at + 1) * span, :]


def unsorted_span(order_ref, sorted_ref, at):
    span = sorted_ref.shape[0] // order_ref.shape[0]
    start = pl.multiple_of(order_ref[at] * span, span)
    return sorted_ref[pl.ds(start, span), :]


def causal(scores, first_row):
    row = lax.broadcasted_iota(jnp.int32, scores.shape, 0) + first_row
    column = lax.broadcasted_iota(jnp.int32, scores.shape, 1)
    return jnp.where(column <= row, scores, -1e30)


def forward_kernel(order_ref, q_ref, k_ref, v_ref, out_ref, log_ref, peak_ref, q_s, k_s, v_s, o_s):
    length = q_ref.shape[0]
    block = min(ROWS, length)
    scale = HEAD_DIM ** (-0.5)
    for source, held in ((q_ref, q_s), (k_ref, k_s), (v_ref, v_s)):
        sort_spans(order_ref, source, held)
    lane = lax.broadcasted_iota(jnp.int32, (block, PAIR), 1)
    peaks = [None, None]
    for start in range(0, length, block):
        end = start + block
        query, key, value = q_s[start:end, :], k_s[:end, :], v_s[:end, :]
        attended, logs = [], []
        for head in range(2):
            mine = (lane // HEAD_DIM) == head
            scores = causal(dot_rt(jnp.where(mine, query, 0), key) * scale, start)
            row_max = jnp.max(scores, 1, keepdims=True)
            terms = jnp.exp(scores - row_max)
            total = jnp.sum(terms, 1, keepdims=True)
            attended.append(dot((terms * (1.0 / total)).astype(bf16), value))
            logs.append(row_max + jnp.log(total))
            top = jnp.max(row_max)
            peaks[head] = top if peaks[head] is None else jnp.maximum(peaks[head], top)
        o_s[start:end, :] = jnp.where(lane < HEAD_DIM, attended[0], attended[1])
        log_ref[0, start:end, :] = jnp.where(lane < HEAD_DIM, logs[0], logs[1])
    for at in range(order_ref.shape[0]):
        span = length // order_ref.shape[0]
        out_ref[at * span : (at + 1) * span, :] = unsorted_span(order_ref, o_s, at).astype(bf16)
    lane = lax.broadcasted_iota(jnp.int32, peak_ref.shape, 2)
    peak_ref[...] = jnp.where(lane < HEAD_DIM, peaks[0], peaks[1])


def attend(order, qkv):
    length = qkv.shape[0]
    pairs = qkv.shape[1] // (3 * PAIR)
    column = lambda first: pl.BlockSpec((length, PAIR), lambda g, order: (0, first + g))
    return pl.pallas_call(
        forward_kernel,
        grid_spec=pltpu.PrefetchScalarGridSpec(
            num_scalar_prefetch=1,
            grid=(pairs,),
            in_specs=[column(0), column(pairs), column(2 * pairs)],
            out_specs=(
                column(0),
                pl.BlockSpec((1, length, PAIR), lambda g, order: (g, 0, 0)),
                pl.BlockSpec((1, 8, PAIR), lambda g, order: (g, 0, 0)),
            ),
            scratch_shapes=[pltpu.VMEM((length, PAIR), bf16)] * 3 + [pltpu.VMEM((length, PAIR), f32)],
        ),
        out_shape=(
            jax.ShapeDtypeStruct((length, pairs * PAIR), bf16),
            jax.ShapeDtypeStruct((pairs, length, PAIR), f32),
            jax.ShapeDtypeStruct((pairs, 8, PAIR), f32),
        ),
        compiler_params=pltpu.CompilerParams(vmem_limit_bytes=VMEM_LIMIT),
        cost_estimate=pl.CostEstimate(
            flops=2 * pairs * length * length * PAIR,
            bytes_accessed=8 * pairs * length * PAIR,
            transcendentals=pairs * length,
        ),
        name="attend",
    )(order, qkv, qkv, qkv)


def backward_kernel(
    order_ref, q_ref, k_ref, v_ref, g_ref, log_ref, cosine_ref, sine_ref, out_ref, *held
):
    q_s, k_s, v_s, g_s, dq_s, dk_s, dv_s = held
    length = q_ref.shape[0]
    block = min(ROWS, length)
    scale = HEAD_DIM ** (-0.5)
    for source, into in ((q_ref, q_s), (k_ref, k_s), (v_ref, v_s), (g_ref, g_s)):
        sort_spans(order_ref, source, into)
    dk_s[...] = jnp.zeros_like(dk_s)
    dv_s[...] = jnp.zeros_like(dv_s)
    lane = lax.broadcasted_iota(jnp.int32, (block, PAIR), 1)
    for start in range(0, length, block):
        end = start + block
        query, grad = q_s[start:end, :], g_s[start:end, :]
        key, value = k_s[:end, :], v_s[:end, :]
        grad_query = []
        for head in range(2):
            mine = (lane // HEAD_DIM) == head
            query_h = jnp.where(mine, query, 0)
            grad_h = jnp.where(mine, grad, 0)
            log_h = log_ref[0, start:end, head * HEAD_DIM : head * HEAD_DIM + 1]
            scores = causal(dot_rt(query_h, key) * scale, start)
            prob = jnp.exp(scores - log_h)
            grad_prob = dot_rt(grad_h, value)
            delta = jnp.sum(prob * grad_prob, 1, keepdims=True)
            grad_score = (prob * (grad_prob - delta)).astype(bf16)
            grad_query.append(dot(grad_score, key))
            dk_s[:end, :] += dot_lt(grad_score, query_h)
            dv_s[:end, :] += dot_lt(prob.astype(bf16), grad_h)
        dq_s[start:end, :] = jnp.where(lane < HEAD_DIM, grad_query[0], grad_query[1])
    pairs = out_ref.shape[1] // (3 * PAIR)
    column = pl.program_id(0)
    span = length // order_ref.shape[0]
    for at in range(order_ref.shape[0]):
        rows = slice(at * span, (at + 1) * span)
        cosine, sine = cosine_ref[rows, :], sine_ref[rows, :]
        for which, source in enumerate((dq_s, dk_s, dv_s)):
            part = unsorted_span(order_ref, source, at)
            if which < 2:
                part = turn(part * scale, cosine, -sine)
            start = pl.multiple_of((which * pairs + column) * PAIR, PAIR)
            out_ref[rows, pl.ds(start, PAIR)] = part.astype(bf16)


def attend_back(order, qkv, grad, logs, cosine, sine):
    length = qkv.shape[0]
    pairs = qkv.shape[1] // (3 * PAIR)
    column = lambda first: pl.BlockSpec((length, PAIR), lambda g, order: (0, first + g))
    whole = pl.BlockSpec((length, PAIR), lambda g, order: (0, 0))
    return pl.pallas_call(
        backward_kernel,
        grid_spec=pltpu.PrefetchScalarGridSpec(
            num_scalar_prefetch=1,
            grid=(pairs,),
            in_specs=[
                column(0),
                column(pairs),
                column(2 * pairs),
                column(0),
                pl.BlockSpec((1, length, PAIR), lambda g, order: (g, 0, 0)),
                whole,
                whole,
            ],
            out_specs=pl.BlockSpec((length, 3 * pairs * PAIR), lambda g, order: (0, 0)),
            scratch_shapes=[pltpu.VMEM((length, PAIR), bf16)] * 4
            + [pltpu.VMEM((length, PAIR), f32)] * 3,
        ),
        out_shape=jax.ShapeDtypeStruct(qkv.shape, bf16),
        compiler_params=pltpu.CompilerParams(vmem_limit_bytes=VMEM_LIMIT),
        cost_estimate=pl.CostEstimate(
            flops=2 * pairs * length * length * PAIR,
            bytes_accessed=16 * pairs * length * PAIR,
            transcendentals=pairs * length,
        ),
        name="attend_back",
    )(order, qkv, qkv, qkv, grad, logs, cosine, sine)


def on_device(
    block_in,
    span_order,
    attn_gain,
    w_query,
    w_key,
    w_value,
    w_out,
    mlp_gain,
    w_gate,
    w_up,
    w_down,
    clip_limit,
    cotangent,
):
    n_ctx = lax.axis_size("ctx")
    n_fsdp = lax.axis_size("fsdp")
    n_bits = n_fsdp.bit_length() - 1
    c_at = lax.axis_index("ctx")
    f_at = lax.axis_index("fsdp")
    t_at = lax.axis_index("tp")
    row_count, width = block_in.shape[1:]
    span_len = row_count // 2
    feature_block = width // n_fsdp

    def along(tensor, shift):
        if shift % n_ctx == 0:
            return tensor
        return lax.ppermute(tensor, "ctx", [(i, (i + shift) % n_ctx) for i in range(n_ctx)])

    def across(tensor, mask):
        return lax.ppermute(tensor, "fsdp", [(i, i ^ mask) for i in range(n_fsdp)])

    def twin(tensor):
        return lax.ppermute(tensor, "tp", [(0, 1), (1, 0)])

    def after(tensor, *earlier):
        return lax.optimization_barrier((tensor, *earlier))[0]

    def reorder(tensor):
        return jnp.concatenate(
            [
                lax.dynamic_slice_in_dim(tensor, (f_at ^ m) * feature_block, feature_block, -1)
                for m in range(n_fsdp)
            ],
            -1,
        )

    def swap_columns(*tensors, late=()):
        piece = tensors[0].shape[1] // n_ctx
        came = []
        for shift in range(n_ctx):
            start = ((c_at + shift) % n_ctx) * piece
            sent = [lax.dynamic_slice_in_dim(tensor, start, piece, 1) for tensor in tensors]
            came.append(after(along(jnp.concatenate(sent, 1), shift), *late))
        return place(c_at, came, 1, ("down",), bf16)[0]

    def swap_rows(tensor, ways, late=(), waiting=None):
        piece = tensor.shape[0] // n_ctx
        came = []
        for shift in range(n_ctx):
            sent = lax.dynamic_slice_in_dim(tensor, ((c_at + shift) % n_ctx) * piece, piece, 0)
            came.append(after(along(sent, shift), *late))
        if waiting is None:
            return place(c_at, came, len(ways), ways, f32)
        came[1], waiting = lax.optimization_barrier((came[1], waiting))
        return place(c_at, came, len(ways), ways, f32), waiting

    def plane_pieces(tensor, late=()):
        if n_fsdp != 4:
            return [tensor] + [after(across(tensor, m), *late) for m in range(1, n_fsdp)]
        half = tensor.shape[0] // 2
        near_x, near_y = across(tensor, 1), across(tensor, 2)
        far = [across(near_x[:half], 2), across(near_y[half:], 1)]
        pieces = [tensor, near_x, near_y, jnp.concatenate(far, 0)]
        return [after(piece, *late) for piece in pieces]

    def gather_plane(tensor, late=()):
        return jnp.concatenate(plane_pieces(tensor, late), 0)

    def scatter_plane(*tensors, late=()):
        size = tensors[0].shape[0] // n_fsdp

        def block(m):
            parts = [tensor[m * size : (m + 1) * size] for tensor in tensors]
            return jnp.concatenate(parts, 1) if len(parts) > 1 else parts[0]

        total = block(0).astype(f32)
        for m in range(1, n_fsdp):
            total = total + after(across(block(m), m), *late).astype(f32)
        return total.astype(bf16)

    def gather_tokens(own):
        return lax.all_gather(own, ("ctx", "tp"), axis=0, tiled=True)

    def scatter_tokens(partial):
        return lax.psum_scatter(partial.astype(bf16), ("ctx", "tp"), scatter_dimension=0, tiled=True)

    order_row = span_order[0]
    positions = (
        order_row[:, None] * span_len + jnp.arange(span_len, dtype=jnp.int32)[None, :]
    ).reshape(-1)
    cosine, sine = rope_tables(positions)
    length = positions.shape[0]

    def own_rows(tensor):
        return reorder(lax.dynamic_slice_in_dim(tensor[0], t_at * span_len, span_len, 0))

    inputs_own = own_rows(block_in)
    cot_own = own_rows(cotangent)

    gains = jnp.stack([attn_gain, mlp_gain])
    gains = gather_plane_small(swap_small(gains, along, c_at, n_ctx), across, n_bits)
    gains_wide = gains.astype(f32)
    gain_one, gain_two = gains_wide[0], gains_wide[1]

    heads_width = w_query.shape[1] // n_ctx
    attn_part = after(swap_columns(w_query, w_key, w_value, w_out.T), gains)
    attn_pieces = plane_pieces(attn_part)
    attn_full = jnp.concatenate(attn_pieces, 0)
    inputs_low = after(gather_tokens(after(inputs_own, attn_part)), attn_full)
    qkv_full = attn_full[:, : 3 * heads_width]
    out_full = attn_full[:, 3 * heads_width :]

    heads_here = heads_width // HEAD_DIM
    normed_one, qkv = project(
        inputs_low, gain_one[None], cosine, sine, attn_pieces, heads_width, row_count
    )
    gate_part = swap_columns(after(w_gate, inputs_low), late=(qkv,))
    up_part = swap_columns(after(w_up, inputs_low), late=(qkv,))
    qkv = after(qkv, gate_part)
    attn_low, log_total, peaks = attend(order_row, qkv)
    down_part = swap_columns(after(w_down.T, up_part))
    gate_full = gather_plane(gate_part, late=(attn_low,))
    up_full = gather_plane(after(up_part, gate_full))
    down_full = gather_plane(after(down_part, up_full))
    attn_low = after(attn_low, up_part, gate_full)
    head_max = peaks[:, 0, ::HEAD_DIM].reshape(-1)
    attn_sum = scatter_tokens(dot_rt(attn_low, out_full))
    attn_sum = after(attn_sum, down_part, up_full)

    inputs_mine = inputs_own.astype(f32)
    resid = inputs_mine + attn_sum.astype(f32)
    inv_two = lax.rsqrt(jnp.mean(resid * resid, -1, keepdims=True) + NORM_EPS)
    scaled_two = resid * inv_two
    normed_mine = (scaled_two * gain_two).astype(bf16)
    normed_two = gather_tokens(normed_mine)
    cot_all = gather_tokens(after(cot_own, normed_mine))
    normed_two = after(normed_two, down_full)
    gate_act = dot(normed_two, gate_full)
    up_act = dot(normed_two, up_full)
    sig_gate = jax.nn.sigmoid(gate_act)
    silu_gate = gate_act * sig_gate
    hidden = (silu_gate * up_act).astype(bf16)
    mlp_partial = dot_rt(hidden, down_full).astype(bf16)
    mlp_sum = scatter_tokens(mlp_partial)
    grad_hidden = dot(after(cot_all, mlp_partial), down_full)
    silu_slope = sig_gate * (1.0 + gate_act * (1.0 - sig_gate))
    grad_gate = (grad_hidden * up_act * silu_slope).astype(bf16)
    grad_up = (grad_hidden * silu_gate).astype(bf16)
    back_two = (dot_rt(grad_gate, gate_full) + dot_rt(grad_up, up_full)).astype(bf16)
    hidden_late, gate_late, up_late = (after(g, back_two) for g in (hidden, grad_gate, grad_up))
    grad_w_down = dot_lt(cot_all, hidden_late).astype(bf16)
    back_two, mlp_sum = lax.optimization_barrier((back_two, mlp_sum))
    grad_normed_two = scatter_tokens(back_two)
    grad_w_gate = dot_lt(normed_two, gate_late).astype(bf16)
    grad_w_up = dot_lt(normed_two, up_late).astype(bf16)
    down_sum = scatter_plane(grad_w_down)
    grad_normed_two = after(grad_normed_two, down_sum, grad_w_gate, grad_w_up).astype(f32)

    grad_gain_two = jnp.sum(grad_normed_two * scaled_two, axis=0)
    weighted_two = grad_normed_two * gain_two
    grad_resid = cot_own.astype(f32) + inv_two * (
        weighted_two - scaled_two * jnp.mean(weighted_two * scaled_two, -1, keepdims=True)
    )
    grad_low = gather_tokens(grad_resid.astype(bf16))
    gate_sum = scatter_plane(after(grad_w_gate, down_sum))
    (down_out,) = swap_rows(down_sum, ("turned",))
    grad_low = after(grad_low, gate_sum, down_out)
    block_out_mine = (resid + mlp_sum.astype(f32)).astype(bf16)

    grad_attended = dot(grad_low, out_full).astype(bf16)
    grad_proj = attend_back(order_row, qkv, grad_attended, log_total, cosine, sine)
    up_sum = scatter_plane(after(grad_w_up, gate_sum), late=(grad_proj,))
    (gate_out,) = swap_rows(after(gate_sum, grad_low), ("side",), late=(grad_proj,))
    back_one = dot_rt(after(grad_proj, up_sum, gate_out), qkv_full).astype(bf16)
    grad_normed_one = scatter_tokens(back_one)
    proj_late, attn_late, back_late = (after(g, back_one) for g in (grad_proj, attn_low, back_one))
    grad_w_qkv = dot_lt(normed_one, proj_late).astype(bf16)
    grad_w_out = dot_lt(grad_low, attn_late).astype(bf16)
    (up_out,) = swap_rows(after(up_sum, back_one), ("side",))
    attn_weight_sum = scatter_plane(grad_w_qkv, grad_w_out, late=(up_out,))
    inputs = inputs_low.astype(f32)
    inv_one = lax.rsqrt(jnp.mean(inputs * inputs, -1, keepdims=True) + NORM_EPS)
    back_late = after(back_late, grad_w_qkv, grad_w_out)
    grad_gain_one = jnp.sum(back_late.astype(f32) * (inputs * inv_one), axis=0)
    grad_normed_one = after(grad_normed_one, grad_w_qkv, grad_w_out).astype(f32)

    inv_mine = lax.rsqrt(jnp.mean(inputs_mine * inputs_mine, -1, keepdims=True) + NORM_EPS)
    scaled_one = inputs_mine * inv_mine
    weighted_one = grad_normed_one * gain_one
    input_grad_mine = grad_resid + inv_mine * (
        weighted_one - scaled_one * jnp.mean(weighted_one * scaled_one, -1, keepdims=True)
    )

    (query_out, key_out, value_out, out_proj_out), gain_grads = swap_rows(
        attn_weight_sum,
        ("side", "side", "side", "turned"),
        waiting=jnp.stack([grad_gain_one, grad_gain_two]),
    )
    gain_grads = gain_grads + twin(gain_grads)
    peak = head_max[None]
    held = {m: gain_grads[:, m * feature_block : (m + 1) * feature_block] for m in range(n_fsdp)}
    for bit in [1 << step for step in range(n_bits)]:
        kept = [m for m in sorted(held) if not m & bit]
        sent = [held[m | bit].reshape(1, -1) for m in kept]
        came = across(jnp.concatenate(sent + [peak], 1), bit)
        size = 2 * feature_block
        held = {
            m: held[m] + came[:, at * size : (at + 1) * size].reshape(2, feature_block)
            for at, m in enumerate(kept)
        }
        peak = jnp.maximum(peak, came[:, len(kept) * size :])
    piece = feature_block // n_ctx
    gain_total = None
    head_peak = jnp.zeros((n_ctx * heads_here,), f32)
    for shift in range(n_ctx):
        sent = lax.dynamic_slice_in_dim(held[0], ((c_at + shift) % n_ctx) * piece, piece, 1)
        came = along(jnp.concatenate([sent.reshape(1, -1), peak], 1), shift)
        part = came[:, : 2 * piece].reshape(2, piece)
        gain_total = part if gain_total is None else gain_total + part
        head_peak = lax.dynamic_update_slice_in_dim(
            head_peak, came[0, 2 * piece :], ((c_at - shift) % n_ctx) * heads_here, 0
        )

    def both_cores(mine):
        mine = reorder(mine)
        other = twin(mine)
        first = jnp.where(t_at == 0, mine, other)
        second = jnp.where(t_at == 0, other, mine)
        return jnp.concatenate([first, second], 0)[None]

    factor = jnp.sqrt(clip_limit / jnp.maximum(clip_limit, head_peak))
    column_factor = jnp.repeat(factor, HEAD_DIM)
    clipped_query = w_query.astype(f32) * column_factor[None, :]
    clipped_key = w_key.astype(f32) * column_factor[None, :]
    return (
        both_cores(block_out_mine),
        both_cores(input_grad_mine),
        gain_total[0],
        query_out,
        key_out,
        value_out,
        out_proj_out,
        gain_total[1],
        gate_out,
        up_out,
        down_out,
        head_peak,
        clipped_query,
        clipped_key,
    )


def swap_small(gains, along, c_at, n_ctx):
    piece = gains.shape[1]
    placed = jnp.zeros((gains.shape[0], piece * n_ctx), gains.dtype)
    for shift in range(n_ctx):
        placed = lax.dynamic_update_slice_in_dim(
            placed, along(gains, shift), ((c_at - shift) % n_ctx) * piece, 1
        )
    return placed


def gather_plane_small(gains, across, n_bits):
    for step in range(n_bits):
        gains = jnp.concatenate([gains, across(gains, 1 << step)], 1)
    return gains


def solution(mesh):
    placed = (
        P("fsdp", "ctx", None),
        P("fsdp", None),
        P(("fsdp", "ctx")),
        P(("fsdp", "ctx"), "tp"),
        P(("fsdp", "ctx"), "tp"),
        P(("fsdp", "ctx"), "tp"),
        P("tp", ("fsdp", "ctx")),
        P(("fsdp", "ctx")),
        P(("fsdp", "ctx"), "tp"),
        P(("fsdp", "ctx"), "tp"),
        P("tp", ("fsdp", "ctx")),
        P("tp"),
        P("fsdp", "ctx", None),
    )
    return jax.shard_map(
        on_device,
        mesh=mesh,
        in_specs=placed,
        out_specs=(
            P("fsdp", "ctx", None),
            P("fsdp", "ctx", None),
            P(("fsdp", "ctx")),
            P(("fsdp", "ctx"), "tp"),
            P(("fsdp", "ctx"), "tp"),
            P(("fsdp", "ctx"), "tp"),
            P("tp", ("fsdp", "ctx")),
            P(("fsdp", "ctx")),
            P(("fsdp", "ctx"), "tp"),
            P(("fsdp", "ctx"), "tp"),
            P("tp", ("fsdp", "ctx")),
            P("tp"),
            P(("fsdp", "ctx"), "tp"),
            P(("fsdp", "ctx"), "tp"),
        ),
        check_vma=False,
    )
```

```python
import functools

import jax
import jax.numpy as jnp
from jax import lax
from jax.experimental import pallas as pl
from jax.experimental.pallas import tpu as pltpu
from jax.sharding import PartitionSpec as P

HEAD_DIM = 64
NORM_EPS = 1e-05
ROPE_BASE = 130000.0

f32 = jnp.float32
bf16 = jnp.bfloat16

PAIR = 2 * HEAD_DIM
ROWS = 256
VMEM_LIMIT = 48 * 1024 * 1024


def rope_tables(positions):
    half_dim = HEAD_DIM // 2
    step_index = jnp.arange(half_dim, dtype=f32)
    frequency = jnp.power(ROPE_BASE, -2.0 * step_index / (2 * half_dim))
    angles = positions.astype(f32)[:, None] * frequency[None, :]
    cosine, sine = jnp.cos(angles), jnp.sin(angles)
    return (
        jnp.concatenate([cosine, cosine, cosine, cosine], 1),
        jnp.concatenate([-sine, sine, -sine, sine], 1),
    )


def dot(left, right):
    return jnp.dot(left, right, preferred_element_type=f32)


def dot_lt(left, right):
    return lax.dot_general(left, right, (((0,), (0,)), ((), ())), preferred_element_type=f32)


def dot_rt(left, right):
    return lax.dot_general(left, right, (((1,), (1,)), ((), ())), preferred_element_type=f32)


def place_kernel(count, ways, at_ref, *refs):
    pieces = len(refs) - count
    slot = lax.rem(at_ref[0] + pieces - pl.program_id(0), pieces)
    for at in range(pieces):

        @pl.when(slot == at)
        def _(source=refs[at]):
            columns = source.shape[1] // count
            for which in range(count):
                part = source[:, which * columns : (which + 1) * columns]
                target = refs[pieces + which]
                part = part.astype(target.dtype)
                target[...] = part.T if ways[which] == "turned" else part


def place(at, pieces, count, ways, dtype):
    slots = len(pieces)
    rows, columns = pieces[0].shape
    columns = columns // count
    shapes = {
        "down": ((slots * rows, columns), (rows, columns), lambda b, at: (b, 0)),
        "side": ((rows, slots * columns), (rows, columns), lambda b, at: (0, b)),
        "turned": ((slots * columns, rows), (columns, rows), lambda b, at: (b, 0)),
    }
    return pl.pallas_call(
        functools.partial(place_kernel, count, ways),
        grid_spec=pltpu.PrefetchScalarGridSpec(
            num_scalar_prefetch=1,
            grid=(slots,),
            in_specs=[pl.BlockSpec(piece.shape, lambda b, at: (0, 0)) for piece in pieces],
            out_specs=[pl.BlockSpec(shapes[way][1], shapes[way][2]) for way in ways],
        ),
        out_shape=[jax.ShapeDtypeStruct(shapes[way][0], dtype) for way in ways],
        compiler_params=pltpu.CompilerParams(vmem_limit_bytes=VMEM_LIMIT),
        cost_estimate=pl.CostEstimate(
            flops=0, bytes_accessed=6 * slots * rows * columns * count, transcendentals=0
        ),
        name="place",
    )(at.astype(jnp.int32)[None], *pieces)


def turn(pair, cosine, sine):
    lane = lax.broadcasted_iota(jnp.int32, pair.shape, 1)
    half_dim = HEAD_DIM // 2
    swapped = jnp.where(
        lane % HEAD_DIM < half_dim,
        pltpu.roll(pair, PAIR - half_dim, 1),
        pltpu.roll(pair, half_dim, 1),
    )
    return pair * cosine + swapped * sine


def project_kernel(pieces, heads_width, x_ref, gain_ref, cosine_ref, sine_ref, *refs):
    weights, normed_ref, out_ref = refs[:pieces], refs[pieces], refs[pieces + 1]
    inputs = x_ref[...].astype(f32)
    inverse = lax.rsqrt(jnp.mean(inputs * inputs, -1, keepdims=True) + NORM_EPS)
    normed = (inputs * inverse * gain_ref[...]).astype(bf16)
    normed_ref[...] = normed
    block = normed.shape[1] // pieces
    proj = None
    for at, weight in enumerate(weights):
        term = dot(normed[:, at * block : (at + 1) * block], weight[:, : 3 * heads_width])
        proj = term if proj is None else proj + term
    cosine, sine = cosine_ref[...], sine_ref[...]
    for at in range(3 * heads_width // PAIR):
        pair = proj[:, at * PAIR : (at + 1) * PAIR]
        if at < 2 * heads_width // PAIR:
            pair = turn(pair, cosine, sine)
        out_ref[:, at * PAIR : (at + 1) * PAIR] = pair.astype(bf16)


def project(tokens, gain, cosine, sine, weights, heads_width, row_block):
    length, width = tokens.shape
    rows = lambda columns: pl.BlockSpec((row_block, columns), lambda i: (i, 0))
    whole = lambda tensor: pl.BlockSpec(tensor.shape, lambda i: (0, 0))
    return pl.pallas_call(
        functools.partial(project_kernel, len(weights), heads_width),
        grid=(length // row_block,),
        out_shape=(
            jax.ShapeDtypeStruct((length, width), bf16),
            jax.ShapeDtypeStruct((length, 3 * heads_width), bf16),
        ),
        in_specs=[rows(width), whole(gain), rows(PAIR), rows(PAIR)] + [whole(w) for w in weights],
        out_specs=(rows(width), rows(3 * heads_width)),
        compiler_params=pltpu.CompilerParams(vmem_limit_bytes=VMEM_LIMIT),
        cost_estimate=pl.CostEstimate(
            flops=length * width * heads_width,
            bytes_accessed=4 * length * width + 8 * width * heads_width,
            transcendentals=length,
        ),
        name="project",
    )(tokens, gain, cosine, sine, *weights)


def sort_spans(order_ref, source, sorted_ref):
    span = sorted_ref.shape[0] // order_ref.shape[0]
    for at in range(order_ref.shape[0]):
        start = pl.multiple_of(order_ref[at] * span, span)
        sorted_ref[pl.ds(start, span), :] = source[at * span : (at + 1) * span, :]


def unsorted_span(order_ref, sorted_ref, at):
    span = sorted_ref.shape[0] // order_ref.shape[0]
    start = pl.multiple_of(order_ref[at] * span, span)
    return sorted_ref[pl.ds(start, span), :]


def causal(scores, first_row):
    row = lax.broadcasted_iota(jnp.int32, scores.shape, 0) + first_row
    column = lax.broadcasted_iota(jnp.int32, scores.shape, 1)
    return jnp.where(column <= row, scores, -1e30)


def forward_kernel(order_ref, q_ref, k_ref, v_ref, out_ref, log_ref, peak_ref, q_s, k_s, v_s, o_s):
    length = q_ref.shape[0]
    block = min(ROWS, length)
    scale = HEAD_DIM ** (-0.5)
    for source, held in ((q_ref, q_s), (k_ref, k_s), (v_ref, v_s)):
        sort_spans(order_ref, source, held)
    lane = lax.broadcasted_iota(jnp.int32, (block, PAIR), 1)
    peaks = [None, None]
    for start in range(0, length, block):
        end = start + block
        query, key, value = q_s[start:end, :], k_s[:end, :], v_s[:end, :]
        attended, logs = [], []
        for head in range(2):
            mine = (lane // HEAD_DIM) == head
            scores = causal(dot_rt(jnp.where(mine, query, 0), key) * scale, start)
            row_max = jnp.max(scores, 1, keepdims=True)
            terms = jnp.exp(scores - row_max)
            total = jnp.sum(terms, 1, keepdims=True)
            attended.append(dot((terms * (1.0 / total)).astype(bf16), value))
            logs.append(row_max + jnp.log(total))
            top = jnp.max(row_max)
            peaks[head] = top if peaks[head] is None else jnp.maximum(peaks[head], top)
        o_s[start:end, :] = jnp.where(lane < HEAD_DIM, attended[0], attended[1])
        log_ref[0, start:end, :] = jnp.where(lane < HEAD_DIM, logs[0], logs[1])
    for at in range(order_ref.shape[0]):
        span = length // order_ref.shape[0]
        out_ref[at * span : (at + 1) * span, :] = unsorted_span(order_ref, o_s, at).astype(bf16)
    lane = lax.broadcasted_iota(jnp.int32, peak_ref.shape, 2)
    peak_ref[...] = jnp.where(lane < HEAD_DIM, peaks[0], peaks[1])


def attend(order, qkv):
    length = qkv.shape[0]
    pairs = qkv.shape[1] // (3 * PAIR)
    column = lambda first: pl.BlockSpec((length, PAIR), lambda g, order: (0, first + g))
    return pl.pallas_call(
        forward_kernel,
        grid_spec=pltpu.PrefetchScalarGridSpec(
            num_scalar_prefetch=1,
            grid=(pairs,),
            in_specs=[column(0), column(pairs), column(2 * pairs)],
            out_specs=(
                column(0),
                pl.BlockSpec((1, length, PAIR), lambda g, order: (g, 0, 0)),
                pl.BlockSpec((1, 8, PAIR), lambda g, order: (g, 0, 0)),
            ),
            scratch_shapes=[pltpu.VMEM((length, PAIR), bf16)] * 3 + [pltpu.VMEM((length, PAIR), f32)],
        ),
        out_shape=(
            jax.ShapeDtypeStruct((length, pairs * PAIR), bf16),
            jax.ShapeDtypeStruct((pairs, length, PAIR), f32),
            jax.ShapeDtypeStruct((pairs, 8, PAIR), f32),
        ),
        compiler_params=pltpu.CompilerParams(vmem_limit_bytes=VMEM_LIMIT),
        cost_estimate=pl.CostEstimate(
            flops=2 * pairs * length * length * PAIR,
            bytes_accessed=8 * pairs * length * PAIR,
            transcendentals=pairs * length,
        ),
        name="attend",
    )(order, qkv, qkv, qkv)


def backward_kernel(
    order_ref, q_ref, k_ref, v_ref, g_ref, log_ref, cosine_ref, sine_ref, out_ref, *held
):
    q_s, k_s, v_s, g_s, dq_s, dk_s, dv_s = held
    length = q_ref.shape[0]
    block = min(ROWS, length)
    scale = HEAD_DIM ** (-0.5)
    for source, into in ((q_ref, q_s), (k_ref, k_s), (v_ref, v_s), (g_ref, g_s)):
        sort_spans(order_ref, source, into)
    dk_s[...] = jnp.zeros_like(dk_s)
    dv_s[...] = jnp.zeros_like(dv_s)
    lane = lax.broadcasted_iota(jnp.int32, (block, PAIR), 1)
    for start in range(0, length, block):
        end = start + block
        query, grad = q_s[start:end, :], g_s[start:end, :]
        key, value = k_s[:end, :], v_s[:end, :]
        grad_query = []
        for head in range(2):
            mine = (lane // HEAD_DIM) == head
            query_h = jnp.where(mine, query, 0)
            grad_h = jnp.where(mine, grad, 0)
            log_h = log_ref[0, start:end, head * HEAD_DIM : head * HEAD_DIM + 1]
            scores = causal(dot_rt(query_h, key) * scale, start)
            prob = jnp.exp(scores - log_h)
            grad_prob = dot_rt(grad_h, value)
            delta = jnp.sum(prob * grad_prob, 1, keepdims=True)
            grad_score = (prob * (grad_prob - delta)).astype(bf16)
            grad_query.append(dot(grad_score, key))
            dk_s[:end, :] += dot_lt(grad_score, query_h)
            dv_s[:end, :] += dot_lt(prob.astype(bf16), grad_h)
        dq_s[start:end, :] = jnp.where(lane < HEAD_DIM, grad_query[0], grad_query[1])
    pairs = out_ref.shape[1] // (3 * PAIR)
    column = pl.program_id(0)
    span = length // order_ref.shape[0]
    for at in range(order_ref.shape[0]):
        rows = slice(at * span, (at + 1) * span)
        cosine, sine = cosine_ref[rows, :], sine_ref[rows, :]
        for which, source in enumerate((dq_s, dk_s, dv_s)):
            part = unsorted_span(order_ref, source, at)
            if which < 2:
                part = turn(part * scale, cosine, -sine)
            start = pl.multiple_of((which * pairs + column) * PAIR, PAIR)
            out_ref[rows, pl.ds(start, PAIR)] = part.astype(bf16)


def attend_back(order, qkv, grad, logs, cosine, sine):
    length = qkv.shape[0]
    pairs = qkv.shape[1] // (3 * PAIR)
    column = lambda first: pl.BlockSpec((length, PAIR), lambda g, order: (0, first + g))
    whole = pl.BlockSpec((length, PAIR), lambda g, order: (0, 0))
    return pl.pallas_call(
        backward_kernel,
        grid_spec=pltpu.PrefetchScalarGridSpec(
            num_scalar_prefetch=1,
            grid=(pairs,),
            in_specs=[
                column(0),
                column(pairs),
                column(2 * pairs),
                column(0),
                pl.BlockSpec((1, length, PAIR), lambda g, order: (g, 0, 0)),
                whole,
                whole,
            ],
            out_specs=pl.BlockSpec((length, 3 * pairs * PAIR), lambda g, order: (0, 0)),
            scratch_shapes=[pltpu.VMEM((length, PAIR), bf16)] * 4
            + [pltpu.VMEM((length, PAIR), f32)] * 3,
        ),
        out_shape=jax.ShapeDtypeStruct(qkv.shape, bf16),
        compiler_params=pltpu.CompilerParams(vmem_limit_bytes=VMEM_LIMIT),
        cost_estimate=pl.CostEstimate(
            flops=2 * pairs * length * length * PAIR,
            bytes_accessed=16 * pairs * length * PAIR,
            transcendentals=pairs * length,
        ),
        name="attend_back",
    )(order, qkv, qkv, qkv, grad, logs, cosine, sine)


def on_device(
    block_in,
    span_order,
    attn_gain,
    w_query,
    w_key,
    w_value,
    w_out,
    mlp_gain,
    w_gate,
    w_up,
    w_down,
    clip_limit,
    cotangent,
):
    n_ctx = lax.axis_size("ctx")
    n_fsdp = lax.axis_size("fsdp")
    n_bits = n_fsdp.bit_length() - 1
    c_at = lax.axis_index("ctx")
    f_at = lax.axis_index("fsdp")
    t_at = lax.axis_index("tp")
    row_count, width = block_in.shape[1:]
    span_len = row_count // 2
    feature_block = width // n_fsdp

    def along(tensor, shift):
        if shift % n_ctx == 0:
            return tensor
        return lax.ppermute(tensor, "ctx", [(i, (i + shift) % n_ctx) for i in range(n_ctx)])

    def across(tensor, mask):
        return lax.ppermute(tensor, "fsdp", [(i, i ^ mask) for i in range(n_fsdp)])

    def twin(tensor):
        return lax.ppermute(tensor, "tp", [(0, 1), (1, 0)])

    def after(tensor, *earlier):
        return lax.optimization_barrier((tensor, *earlier))[0]

    def reorder(tensor):
        return jnp.concatenate(
            [
                lax.dynamic_slice_in_dim(tensor, (f_at ^ m) * feature_block, feature_block, -1)
                for m in range(n_fsdp)
            ],
            -1,
        )

    def swap_columns(*tensors, late=()):
        piece = tensors[0].shape[1] // n_ctx
        came = []
        for shift in range(n_ctx):
            start = ((c_at + shift) % n_ctx) * piece
            sent = [lax.dynamic_slice_in_dim(tensor, start, piece, 1) for tensor in tensors]
            came.append(after(along(jnp.concatenate(sent, 1), shift), *late))
        return place(c_at, came, 1, ("down",), bf16)[0]

    def swap_rows(tensor, ways, late=()):
        piece = tensor.shape[0] // n_ctx
        came = []
        for shift in range(n_ctx):
            sent = lax.dynamic_slice_in_dim(tensor, ((c_at + shift) % n_ctx) * piece, piece, 0)
            came.append(after(along(sent, shift), *late))
        return place(c_at, came, len(ways), ways, f32)

    def plane_pieces(tensor, late=()):
        if n_fsdp != 4:
            return [tensor] + [after(across(tensor, m), *late) for m in range(1, n_fsdp)]
        half = tensor.shape[0] // 2
        near_x, near_y = across(tensor, 1), across(tensor, 2)
        far = [across(near_x[:half], 2), across(near_y[half:], 1)]
        pieces = [tensor, near_x, near_y, jnp.concatenate(far, 0)]
        return [after(piece, *late) for piece in pieces]

    def gather_plane(tensor, late=()):
        return jnp.concatenate(plane_pieces(tensor, late), 0)

    def scatter_plane(*tensors, late=()):
        size = tensors[0].shape[0] // n_fsdp

        def block(m):
            parts = [tensor[m * size : (m + 1) * size] for tensor in tensors]
            return jnp.concatenate(parts, 1) if len(parts) > 1 else parts[0]

        total = block(0).astype(f32)
        for m in range(1, n_fsdp):
            total = total + after(across(block(m), m), *late).astype(f32)
        return total.astype(bf16)

    def gather_tokens(own):
        return lax.all_gather(own, ("ctx", "tp"), axis=0, tiled=True)

    def scatter_tokens(partial):
        return lax.psum_scatter(partial.astype(bf16), ("ctx", "tp"), scatter_dimension=0, tiled=True)

    order_row = span_order[0]
    positions = (
        order_row[:, None] * span_len + jnp.arange(span_len, dtype=jnp.int32)[None, :]
    ).reshape(-1)
    cosine, sine = rope_tables(positions)
    length = positions.shape[0]

    def own_rows(tensor):
        return reorder(lax.dynamic_slice_in_dim(tensor[0], t_at * span_len, span_len, 0))

    inputs_own = own_rows(block_in)
    cot_own = own_rows(cotangent)

    gains = jnp.stack([attn_gain, mlp_gain])
    gains = gather_plane_small(swap_small(gains, along, c_at, n_ctx), across, n_bits)
    gains_wide = gains.astype(f32)
    gain_one, gain_two = gains_wide[0], gains_wide[1]

    heads_width = w_query.shape[1] // n_ctx
    attn_part = after(swap_columns(w_query, w_key, w_value, w_out.T), gains)
    attn_pieces = plane_pieces(attn_part)
    attn_full = jnp.concatenate(attn_pieces, 0)
    inputs_low = after(gather_tokens(after(inputs_own, attn_part)), attn_full)
    qkv_full = attn_full[:, : 3 * heads_width]
    out_full = attn_full[:, 3 * heads_width :]

    heads_here = heads_width // HEAD_DIM
    normed_one, qkv = project(
        inputs_low, gain_one[None], cosine, sine, attn_pieces, heads_width, row_count
    )
    gate_part = swap_columns(after(w_gate, inputs_low), late=(qkv,))
    up_part = swap_columns(after(w_up, inputs_low), late=(qkv,))
    qkv = after(qkv, gate_part)
    attn_low, log_total, peaks = attend(order_row, qkv)
    down_part = swap_columns(after(w_down.T, up_part))
    gate_full = gather_plane(gate_part, late=(attn_low,))
    up_full = gather_plane(after(up_part, gate_full))
    down_full = gather_plane(after(down_part, up_full))
    attn_low = after(attn_low, up_part, gate_full)
    head_max = peaks[:, 0, ::HEAD_DIM].reshape(-1)
    attn_sum = scatter_tokens(dot_rt(attn_low, out_full))
    attn_sum = after(attn_sum, down_part, up_full)

    inputs_mine = inputs_own.astype(f32)
    resid = inputs_mine + attn_sum.astype(f32)
    inv_two = lax.rsqrt(jnp.mean(resid * resid, -1, keepdims=True) + NORM_EPS)
    scaled_two = resid * inv_two
    normed_mine = (scaled_two * gain_two).astype(bf16)
    normed_two = gather_tokens(normed_mine)
    cot_all = gather_tokens(after(cot_own, normed_mine))
    normed_two = after(normed_two, down_full)
    gate_act = dot(normed_two, gate_full)
    up_act = dot(normed_two, up_full)
    sig_gate = jax.nn.sigmoid(gate_act)
    silu_gate = gate_act * sig_gate
    hidden = (silu_gate * up_act).astype(bf16)
    mlp_partial = dot_rt(hidden, down_full).astype(bf16)
    grad_hidden = dot(after(cot_all, mlp_partial), down_full)
    silu_slope = sig_gate * (1.0 + gate_act * (1.0 - sig_gate))
    grad_gate = (grad_hidden * up_act * silu_slope).astype(bf16)
    grad_up = (grad_hidden * silu_gate).astype(bf16)
    back_two = (dot_rt(grad_gate, gate_full) + dot_rt(grad_up, up_full)).astype(bf16)
    hidden_late, gate_late, up_late = (after(g, back_two) for g in (hidden, grad_gate, grad_up))
    grad_w_down = dot_lt(cot_all, hidden_late).astype(bf16)
    grad_normed_two = scatter_tokens(back_two)
    grad_w_gate = dot_lt(normed_two, gate_late).astype(bf16)
    grad_w_up = dot_lt(normed_two, up_late).astype(bf16)
    down_sum = scatter_plane(grad_w_down)
    grad_normed_two = after(grad_normed_two, down_sum, grad_w_gate, grad_w_up).astype(f32)

    grad_gain_two = jnp.sum(grad_normed_two * scaled_two, axis=0)
    weighted_two = grad_normed_two * gain_two
    grad_resid = cot_own.astype(f32) + inv_two * (
        weighted_two - scaled_two * jnp.mean(weighted_two * scaled_two, -1, keepdims=True)
    )
    grad_low = gather_tokens(grad_resid.astype(bf16))
    gate_sum = scatter_plane(after(grad_w_gate, down_sum))
    (down_out,) = swap_rows(down_sum, ("turned",))
    grad_low = after(grad_low, gate_sum, down_out)
    mlp_sum = scatter_tokens(after(mlp_partial, grad_low))

    grad_attended = dot(grad_low, out_full).astype(bf16)
    grad_proj = attend_back(order_row, qkv, grad_attended, log_total, cosine, sine)
    up_sum = scatter_plane(after(grad_w_up, gate_sum), late=(grad_proj,))
    (gate_out,) = swap_rows(after(gate_sum, grad_low), ("side",), late=(grad_proj,))
    back_one = dot_rt(after(grad_proj, up_sum, gate_out), qkv_full).astype(bf16)
    back_one, mlp_sum = lax.optimization_barrier((back_one, mlp_sum))
    block_out_mine = (resid + mlp_sum.astype(f32)).astype(bf16)
    grad_normed_one = scatter_tokens(back_one)
    proj_late, attn_late, back_late = (after(g, back_one) for g in (grad_proj, attn_low, back_one))
    grad_w_qkv = dot_lt(normed_one, proj_late).astype(bf16)
    grad_w_out = dot_lt(grad_low, attn_late).astype(bf16)
    (up_out,) = swap_rows(after(up_sum, back_one), ("side",))
    attn_weight_sum = scatter_plane(grad_w_qkv, grad_w_out, late=(up_out,))
    query_out, key_out, value_out, out_proj_out = swap_rows(
        attn_weight_sum, ("side", "side", "side", "turned")
    )
    inputs = inputs_low.astype(f32)
    inv_one = lax.rsqrt(jnp.mean(inputs * inputs, -1, keepdims=True) + NORM_EPS)
    back_late = after(back_late, grad_w_qkv, grad_w_out)
    grad_gain_one = jnp.sum(back_late.astype(f32) * (inputs * inv_one), axis=0)
    grad_normed_one = after(grad_normed_one, grad_w_qkv, grad_w_out).astype(f32)

    inv_mine = lax.rsqrt(jnp.mean(inputs_mine * inputs_mine, -1, keepdims=True) + NORM_EPS)
    scaled_one = inputs_mine * inv_mine
    weighted_one = grad_normed_one * gain_one
    input_grad_mine = grad_resid + inv_mine * (
        weighted_one - scaled_one * jnp.mean(weighted_one * scaled_one, -1, keepdims=True)
    )

    gain_grads = after(jnp.stack([grad_gain_one, grad_gain_two]), attn_weight_sum)
    gain_grads = gain_grads + twin(gain_grads)
    peak = head_max[None]
    held = {m: gain_grads[:, m * feature_block : (m + 1) * feature_block] for m in range(n_fsdp)}
    for bit in [1 << step for step in range(n_bits)]:
        kept = [m for m in sorted(held) if not m & bit]
        sent = [held[m | bit].reshape(1, -1) for m in kept]
        came = across(jnp.concatenate(sent + [peak], 1), bit)
        size = 2 * feature_block
        held = {
            m: held[m] + came[:, at * size : (at + 1) * size].reshape(2, feature_block)
            for at, m in enumerate(kept)
        }
        peak = jnp.maximum(peak, came[:, len(kept) * size :])
    piece = feature_block // n_ctx
    gain_total = None
    head_peak = jnp.zeros((n_ctx * heads_here,), f32)
    for shift in range(n_ctx):
        sent = lax.dynamic_slice_in_dim(held[0], ((c_at + shift) % n_ctx) * piece, piece, 1)
        came = along(jnp.concatenate([sent.reshape(1, -1), peak], 1), shift)
        part = came[:, : 2 * piece].reshape(2, piece)
        gain_total = part if gain_total is None else gain_total + part
        head_peak = lax.dynamic_update_slice_in_dim(
            head_peak, came[0, 2 * piece :], ((c_at - shift) % n_ctx) * heads_here, 0
        )

    def both_cores(mine):
        mine = reorder(mine)
        other = twin(mine)
        first = jnp.where(t_at == 0, mine, other)
        second = jnp.where(t_at == 0, other, mine)
        return jnp.concatenate([first, second], 0)[None]

    factor = jnp.sqrt(clip_limit / jnp.maximum(clip_limit, head_peak))
    column_factor = jnp.repeat(factor, HEAD_DIM)
    clipped_query = w_query.astype(f32) * column_factor[None, :]
    clipped_key = w_key.astype(f32) * column_factor[None, :]
    return (
        both_cores(block_out_mine),
        both_cores(input_grad_mine),
        gain_total[0],
        query_out,
        key_out,
        value_out,
        out_proj_out,
        gain_total[1],
        gate_out,
        up_out,
        down_out,
        head_peak,
        clipped_query,
        clipped_key,
    )


def swap_small(gains, along, c_at, n_ctx):
    piece = gains.shape[1]
    placed = jnp.zeros((gains.shape[0], piece * n_ctx), gains.dtype)
    for shift in range(n_ctx):
        placed = lax.dynamic_update_slice_in_dim(
            placed, along(gains, shift), ((c_at - shift) % n_ctx) * piece, 1
        )
    return placed


def gather_plane_small(gains, across, n_bits):
    for step in range(n_bits):
        gains = jnp.concatenate([gains, across(gains, 1 << step)], 1)
    return gains


def solution(mesh):
    placed = (
        P("fsdp", "ctx", None),
        P("fsdp", None),
        P(("fsdp", "ctx")),
        P(("fsdp", "ctx"), "tp"),
        P(("fsdp", "ctx"), "tp"),
        P(("fsdp", "ctx"), "tp"),
        P("tp", ("fsdp", "ctx")),
        P(("fsdp", "ctx")),
        P(("fsdp", "ctx"), "tp"),
        P(("fsdp", "ctx"), "tp"),
        P("tp", ("fsdp", "ctx")),
        P("tp"),
        P("fsdp", "ctx", None),
    )
    return jax.shard_map(
        on_device,
        mesh=mesh,
        in_specs=placed,
        out_specs=(
            P("fsdp", "ctx", None),
            P("fsdp", "ctx", None),
            P(("fsdp", "ctx")),
            P(("fsdp", "ctx"), "tp"),
            P(("fsdp", "ctx"), "tp"),
            P(("fsdp", "ctx"), "tp"),
            P("tp", ("fsdp", "ctx")),
            P(("fsdp", "ctx")),
            P(("fsdp", "ctx"), "tp"),
            P(("fsdp", "ctx"), "tp"),
            P("tp", ("fsdp", "ctx")),
            P("tp"),
            P(("fsdp", "ctx"), "tp"),
            P(("fsdp", "ctx"), "tp"),
        ),
        check_vma=False,
    )
```
